128 devices in a mesh: dp: 16 (over y, x_lo, core), fsdp: 8 (over z, x_hi).
Axes of the slice: x: 4 (x_hi: 2, x_lo: 2; x = x_hi * 2 + x_lo), y: 4, z: 4, core: 2. Of those that a mesh axis runs over, the one named last changes fastest.
Arguments:
- q_policy: bfloat16 [32768, 2560], P(('dp', 'fsdp')), may hold values from -288 to 288
- kv_policy: bfloat16 [32768, 1024], P(('dp', 'fsdp')), may hold values from -72 to 72
- q_reference: bfloat16 [32768, 2560], P(('dp', 'fsdp')), may hold values from -288 to 288
- kv_reference: bfloat16 [32768, 1024], P(('dp', 'fsdp')), may hold values from -6 to 6
- target: bfloat16 [32768, 2560], P(('dp', 'fsdp')), may hold values from -4 to 4
- send_slot: int32 [128, 256], P(('dp', 'fsdp')), may hold values from 0 to 255, each once within a row
- lengths: int32 [128, 2], P(('dp', 'fsdp')), may hold values from 1 to 192, 256 in all within a row
- rewards: float32 [256], P(('dp', 'fsdp')), may hold values from -6 to 6
- group_ids: int32 [256], P(('dp', 'fsdp')), may hold values from 0 to 31, as said below
- policy_weight: bfloat16 [2560, 2560], P('fsdp'), may hold values from -6 to 6
- ema_weight: float32 [2560, 2560], P('fsdp'), may hold values from -6 to 6
Outputs:
- update: float32 [2560, 2560], P('fsdp')
- new_weights: bfloat16 [2560, 2560], P('fsdp')
- ema_next: float32 [2560, 2560], P('fsdp')
The draws below stay inside these ranges and needn't reach their ends.
Inputs may be any that keep to these rules, and one draw needn't show every extreme that they name: `send_slot`: each row is a permutation of 0 to 255. Each device's 2 lengths sum to 256. `group_ids`: each prompt names exactly 8 rollouts.
All inputs are finite; a program needn't handle non-finite values.
Results may differ from the reference program's by a relative error of at most 0.02.
Values may be sent and summed in bfloat16 or wider, within the bound.
No kernel may reach another device: no remote copies, remote signals or barrier semaphores. Data moves between devices by JAX's collectives and lax.ppermute only.
A program may use at most 128 MiB of HBM per device.

```python
import math
import jax
import jax.numpy as jnp
import numpy as np
from jax import lax

HEADS = 20
KV_HEADS = 4
HEAD_DIM = 128
D_OUT = 2560
ROWS_DEV = 256
SEQ_DEV = 2
GROUP = 8
Q_WIDTH = 2560
SPAN = 16
MAX_LEN = 192
TOKENS = 32768
ROLLOUTS = 256
GROUPS = 32
N_DP = 16
N_FSDP = 8
DEVICES = 128


def draw_q_policy(key, part):
    key = jax.random.fold_in(key, 5)
    base_key = jax.random.fold_in(key, 0)
    base = jnp.clip(jax.random.normal(base_key, (TOKENS, Q_WIDTH), jnp.float32), -6.0, 6.0)
    return base.astype(jnp.bfloat16)


def draw_q_reference(key, part):
    key = jax.random.fold_in(key, 7)
    base_key = jax.random.fold_in(key, 0)
    base = jnp.clip(jax.random.normal(base_key, (TOKENS, Q_WIDTH), jnp.float32), -6.0, 6.0)
    return base.astype(jnp.bfloat16)


def column_rise(ceiling):
    count = KV_HEADS * HEAD_DIM
    place = jnp.arange(count, dtype=jnp.float32) / (count - 1)
    rising = jnp.exp(math.log(ceiling) * place)
    return jnp.concatenate([jnp.ones((count,), jnp.float32), rising])[None, :]


def draw_kv_policy(key, part):
    key = jax.random.fold_in(key, 13)
    shape = (TOKENS, 2 * KV_HEADS * HEAD_DIM)
    base = jnp.clip(jax.random.normal(key, shape, jnp.float32), -6.0, 6.0)
    return (base * column_rise(6.0)).astype(jnp.bfloat16)


def draw_target(key, part):
    key = jax.random.fold_in(key, 11)
    return jnp.clip(jax.random.normal(key, (TOKENS, D_OUT), jnp.float32), -4.0, 4.0).astype(jnp.bfloat16)


def draw_group_ids(key, part):
    key = jax.random.fold_in(key, 9)
    return (jax.random.permutation(key, ROLLOUTS) // GROUP).astype(jnp.int32)


def level_of(own_key, dims, cuts, least, largest):
    gain = 1.0
    for axis_at, shards_of in cuts:
        draws = jax.random.uniform(jax.random.fold_in(jax.random.fold_in(own_key, 6), axis_at), (shards_of,), jnp.float32, least / len(cuts), largest / len(cuts))
        gain = gain * jnp.repeat(jnp.exp(draws), dims[axis_at] // shards_of).reshape((-1,) + (1,) * (len(dims) - 1 - axis_at))
    return gain


def split_up(amount, total, most, lean):
    portions = [(1 << 20) // math.isqrt(grade ** lean) + 1 for grade in range(2, amount + 1)]
    rest, holding = total - most - (amount - 1), [1] * (amount - 1)
    while rest > 0:
        free = [i for i in range(amount - 1) if holding[i] < most]
        pool, left = sum([portions[i] for i in free]), rest
        for i in free:
            more = min(most - holding[i], max(1, left * portions[i] // pool), rest)
            holding[i] = holding[i] + more
            rest = rest - more
    return np.array([most] + holding)


def ragged(rng, number_of, total, limit, lean):
    if number_of == 2:
        one = jax.random.randint(rng, (), max(1, total - limit), min(limit, total - 1) + 1)
        return jnp.stack([one, total - one])
    tallies = jnp.asarray(split_up(number_of, total, limit, lean), jnp.int32)
    couples = (number_of - 1) // 2
    giver, receiver = tallies[1:1 + 2 * couples:2], tallies[2:2 + 2 * couples:2]
    room = jnp.minimum(giver - 1, limit - receiver)
    passed = jax.random.randint(jax.random.fold_in(rng, 1), (couples,), 0, 1 << 20) % (room + 1)
    tallies = tallies.at[1:1 + 2 * couples:2].set(giver - passed).at[2:2 + 2 * couples:2].set(receiver + passed)
    return tallies[jax.random.permutation(jax.random.fold_in(rng, 2), number_of)]


def gaussian(key, shape, scale, most, cuts=(), kind=jnp.bfloat16):
    values = jax.random.normal(key, shape, jnp.float32) * scale
    if len(cuts) > 0:
        values = level_of(key, shape, cuts, -0.22, 0.18) * values
    return jnp.clip(values, min=-most, max=most).astype(kind)


def setup_inputs(seed: int = 0) -> dict:
    arg_keys = jax.random.split(jax.random.key(seed), 12)
    q_policy = draw_q_policy(jax.random.fold_in(arg_keys[11], 71), 0)
    kv_policy = draw_kv_policy(jax.random.fold_in(arg_keys[11], 71), 0)
    q_reference = draw_q_reference(jax.random.fold_in(arg_keys[11], 71), 0)
    kv_reference = gaussian(arg_keys[3], (TOKENS, 2 * KV_HEADS * HEAD_DIM), 1.0, 6.0, ((0, 128),))
    target = draw_target(jax.random.fold_in(arg_keys[11], 71), 0)
    send_slot = jax.vmap(lambda own: jax.random.permutation(own, ROWS_DEV))(jax.random.split(arg_keys[5], DEVICES)).reshape((DEVICES, ROWS_DEV)).astype(jnp.int32)
    lengths = jax.vmap(lambda own: ragged(own, SEQ_DEV, ROWS_DEV, MAX_LEN, 2))(jax.random.split(arg_keys[6], DEVICES)).reshape((DEVICES, SEQ_DEV)).astype(jnp.int32)
    rewards = gaussian(arg_keys[7], (ROLLOUTS,), 1.0, 6.0, ((0, 128),), jnp.float32)
    group_ids = draw_group_ids(jax.random.fold_in(arg_keys[11], 71), 0)
    policy_weight = gaussian(arg_keys[9], (Q_WIDTH, D_OUT), 1.0, 6.0, ((0, 8),))
    ema_weight = gaussian(arg_keys[10], (Q_WIDTH, D_OUT), 1.0, 6.0, ((0, 8),), jnp.float32)
    return {"q_policy": q_policy, "kv_policy": kv_policy, "q_reference": q_reference, "kv_reference": kv_reference, "target": target, "send_slot": send_slot, "lengths": lengths, "rewards": rewards, "group_ids": group_ids, "policy_weight": policy_weight, "ema_weight": ema_weight}


kl_weight = 0.1
step_size = 0.02
ema_decay = 0.95
std_floor = 0.6
norm_epsilon = 1e-06

def row_layout(lengths_local, row_count):
    places = jnp.arange(row_count, dtype=jnp.int32)
    bounds = jnp.cumsum(lengths_local).astype(jnp.int32)
    segment = lax.optimization_barrier(jnp.sum((places[:, None] >= bounds[None, :]).astype(jnp.int32), axis=1))
    choose = segment[:, None] == jnp.arange(lengths_local.shape[0], dtype=jnp.int32)[None, :]
    return (segment, choose)

def attend(queries, keys_values, segment):
    row_count = queries.shape[0]
    group_size = HEADS // KV_HEADS
    group_width = group_size * HEAD_DIM
    split_at = KV_HEADS * HEAD_DIM
    places = jnp.arange(row_count, dtype=jnp.int32)
    allowed = (places[None, :] <= places[:, None]) & (segment[None, :] == segment[:, None])

    def one_group(head):
        grouped = lax.dynamic_slice_in_dim(queries, head * group_width, group_width, 1)
        grouped = grouped.astype(jnp.float32).reshape(row_count, group_size, HEAD_DIM)
        key_rows = lax.dynamic_slice_in_dim(keys_values, head * HEAD_DIM, HEAD_DIM, 1).astype(jnp.float32)
        value_rows = lax.dynamic_slice_in_dim(keys_values, split_at + head * HEAD_DIM, HEAD_DIM, 1).astype(jnp.float32)
        scores = jnp.einsum('qgd,kd->gqk', grouped, key_rows) / math.sqrt(HEAD_DIM)
        masked = jnp.where(allowed[None, :, :], scores, -1e+30)
        row_peak = lax.optimization_barrier(jnp.max(masked, axis=-1, keepdims=True))
        weights = jnp.where(allowed[None, :, :], jnp.exp(masked - row_peak), 0.0)
        totals = lax.optimization_barrier(jnp.sum(weights, axis=-1, keepdims=True))
        shares = (weights / totals).astype(jnp.bfloat16)
        mixture = jnp.einsum('gqk,kd->qgd', shares.astype(jnp.float32), value_rows)
        return mixture.reshape(row_count, group_width).astype(jnp.bfloat16)
    blocks = lax.map(one_group, jnp.arange(KV_HEADS, dtype=jnp.int32))
    return blocks.transpose(1, 0, 2).reshape(row_count, HEADS * HEAD_DIM)

def advantage_from(rewards, member, first, second):
    center = first / GROUP
    spread = jnp.maximum(jnp.sqrt(jnp.maximum(second / GROUP - center * center, 0.0)), std_floor)
    shifted = rewards - jnp.dot(member, center, precision=lax.Precision.HIGHEST)
    return shifted / jnp.dot(member, spread, precision=lax.Precision.HIGHEST)

def normalize(rows):
    scale = jnp.sqrt(lax.optimization_barrier(jnp.mean(rows * rows, axis=1, keepdims=True)) + norm_epsilon)
    return (rows / scale, scale)

def token_gradient(y_policy, y_reference, target_rows, choose, lengths_local, advantage_local):
    row_length = lax.optimization_barrier(jnp.sum(jnp.where(choose, lengths_local[None, :], 0), axis=1)).astype(jnp.float32)
    row_advantage = lax.optimization_barrier(jnp.sum(jnp.where(choose, advantage_local[None, :], 0.0), axis=1))
    h_policy, norm_policy = normalize(y_policy)
    h_reference, norm_reference = normalize(y_reference)
    target_float = target_rows.astype(jnp.float32)
    gap_policy = h_policy - target_float
    gap_reference = h_reference - target_float
    log_factor = 1.0 / (4.0 * math.sqrt(target_rows.shape[1]))
    log_policy = -lax.optimization_barrier(jnp.sum(gap_policy * gap_policy, axis=1)) * log_factor
    log_reference = -lax.optimization_barrier(jnp.sum(gap_reference * gap_reference, axis=1)) * log_factor
    weight_rows = (row_advantage - kl_weight * (1.0 - jnp.exp(log_reference - log_policy))) / row_length
    along = lax.optimization_barrier(jnp.mean(gap_policy * h_policy, axis=1, keepdims=True))
    grad = weight_rows[:, None] * (gap_policy - h_policy * along) / norm_policy
    return grad.astype(jnp.bfloat16)

def pack(array, send_slot):
    device_count = array.shape[0] // ROWS_DEV
    width = array.shape[1]
    shaped = array.reshape(device_count, ROWS_DEV, width)
    device_rows = jnp.arange(device_count, dtype=jnp.int32)[:, None]
    inverse = jnp.zeros((device_count, ROWS_DEV), jnp.int32).at[device_rows, send_slot].set(jnp.broadcast_to(jnp.arange(ROWS_DEV, dtype=jnp.int32)[None, :], (device_count, ROWS_DEV)))
    ordered = jnp.take_along_axis(shaped, inverse[:, :, None], axis=1)
    spread = ordered.reshape(N_DP, N_FSDP, N_DP, SPAN, width)
    return spread.transpose(2, 1, 0, 3, 4).reshape(N_DP, N_FSDP, ROWS_DEV, width)

def device_term(item, policy_weight, ema_half):
    query_policy, pairs_policy, query_reference, pairs_reference, target_rows, lengths_local, advantage_local = item
    segment, choose = row_layout(lengths_local, ROWS_DEV)
    out_policy = attend(query_policy, pairs_policy, segment)
    out_reference = attend(query_reference, pairs_reference, segment)
    y_policy = jnp.dot(out_policy, policy_weight, preferred_element_type=jnp.float32)
    y_reference = jnp.dot(out_reference, ema_half, preferred_element_type=jnp.float32)
    grad_rows = token_gradient(y_policy, y_reference, target_rows, choose, lengths_local, advantage_local)
    return jnp.dot(out_policy.T, grad_rows, preferred_element_type=jnp.float32)

def reference(q_policy, kv_policy, q_reference, kv_reference, target, send_slot, lengths, rewards, group_ids, policy_weight, ema_weight):
    member = (group_ids[:, None] == jnp.arange(GROUPS, dtype=jnp.int32)[None, :]).astype(jnp.float32)
    first = jnp.dot(rewards, member, precision=lax.Precision.HIGHEST)
    second = jnp.dot(rewards * rewards, member, precision=lax.Precision.HIGHEST)
    advantage = advantage_from(rewards, member, first, second).reshape(N_DP, N_FSDP, SEQ_DEV)
    stacked = (pack(q_policy, send_slot), pack(kv_policy, send_slot), pack(q_reference, send_slot), pack(kv_reference, send_slot), pack(target, send_slot), lengths.reshape(N_DP, N_FSDP, SEQ_DEV), advantage)
    ema_half = ema_weight.astype(jnp.bfloat16)
    empty = jnp.zeros((Q_WIDTH, D_OUT), jnp.float32)

    def outer(running, block):

        def inner(share, item):
            rounded = lax.optimization_barrier(device_term(item, policy_weight, ema_half).astype(jnp.bfloat16))
            return (share + rounded.astype(jnp.float32), None)
        share, unused = lax.scan(inner, empty, block)
        rounded = lax.optimization_barrier(share.astype(jnp.bfloat16))
        return (running + rounded.astype(jnp.float32), None)
    grad_total, unused = lax.scan(outer, empty, stacked)
    mean_square = jnp.mean(grad_total * grad_total)
    update = grad_total / jnp.sqrt(mean_square + norm_epsilon)
    moved = policy_weight.astype(jnp.float32) - step_size * update
    return (update, moved.astype(jnp.bfloat16), ema_decay * ema_weight + (1.0 - ema_decay) * moved)
```

```python
import functools
import math

import jax
import jax.numpy as jnp
from jax import lax
from jax.experimental import pallas as pl
from jax.experimental.pallas import tpu as pltpu
from jax.sharding import Mesh
from jax.sharding import PartitionSpec as P

HEADS = 20
KV_HEADS = 4
HEAD_DIM = 128
D_OUT = 2560
GROUP = 8
Q_WIDTH = 2560
ROWS = 256
SPAN = 16
SHARD = 320
HALF = 1280
CHUNK = 256
PIECE = 640

kl_weight = 0.1
step_size = 0.02
ema_decay = 0.95
std_floor = 0.6
norm_epsilon = 1e-06

bf16 = jnp.bfloat16
f32 = jnp.float32
VMEM = pltpu.VMEM
SMEM = pltpu.SMEM
BIG = pltpu.CompilerParams(vmem_limit_bytes=56 * 1024 * 1024)

DP = ("y", "xl", "c")
FSDP = ("z", "xh")
EVERY = DP + FSDP


def ring(step):
    return [(i, (i + step) % 4) for i in range(4)]


FLIP = [(0, 1), (1, 0)]
ACROSS = [(2, 1), (1, 2), (0, 3), (3, 0)]


def whole(shape=None):
    return pl.BlockSpec(memory_space=VMEM)


def scalars():
    return pl.BlockSpec(memory_space=SMEM)


def in_place():
    return pl.BlockSpec(memory_space=pl.ANY)


def dot(a, b):
    return jnp.dot(a, b, preferred_element_type=f32)


def one_hot_rows(slots_ref):
    return (lax.broadcasted_iota(jnp.int32, (ROWS, ROWS), 0) == slots_ref[...]).astype(bf16)


def pack_policy_kernel(slots_ref, q_ref, kv_ref, out_ref):
    pick = one_hot_rows(slots_ref)
    out_ref[:, :Q_WIDTH] = dot(pick, q_ref[...]).astype(bf16)
    out_ref[:, Q_WIDTH:] = dot(pick, kv_ref[...]).astype(bf16)


def pack_reference_kernel(slots_ref, q_ref, kv_ref, target_ref, facts_ref, out_ref):
    pick = one_hot_rows(slots_ref)
    rows = dot(pick, target_ref[...]).astype(bf16)
    for pair in range(ROWS // (2 * SPAN)):
        top = pair * 2 * SPAN
        first, second = rows[top : top + SPAN], rows[top + SPAN : top + 2 * SPAN]
        out_ref[top : top + SPAN, :HALF] = first[:, :HALF]
        out_ref[top : top + SPAN, HALF:D_OUT] = second[:, :HALF]
        out_ref[top + SPAN : top + 2 * SPAN, :HALF] = first[:, HALF:]
        out_ref[top + SPAN : top + 2 * SPAN, HALF:D_OUT] = second[:, HALF:]
    out_ref[:, D_OUT : D_OUT + Q_WIDTH] = dot(pick, q_ref[...]).astype(bf16)
    out_ref[:, D_OUT + Q_WIDTH : D_OUT + Q_WIDTH + 1024] = dot(pick, kv_ref[...]).astype(bf16)
    facts = facts_ref[...]
    high = facts.astype(bf16).astype(f32)
    middle = (facts - high).astype(bf16).astype(f32)
    low = facts - high - middle
    lane = lax.broadcasted_iota(jnp.int32, facts.shape, 1)
    coded = jnp.where(lane < 8, high, jnp.where(lane < 16, middle, low)).astype(bf16)
    for block in range(ROWS // SPAN):
        out_ref[block * SPAN : (block + 1) * SPAN, D_OUT + Q_WIDTH + 1024 :] = coded


def attention_kernel(lengths_ref, q_ref, k_ref, v_ref, out_ref):
    row = lax.broadcasted_iota(jnp.int32, (ROWS, ROWS), 0)
    column = lax.broadcasted_iota(jnp.int32, (ROWS, ROWS), 1)
    bound = lengths_ref[0, 0]
    allowed = (column <= row) & ((column >= bound) | (row < bound))
    keys, values = k_ref[...], v_ref[...]
    for head in range(HEADS // KV_HEADS):
        lanes = slice(head * HEAD_DIM, (head + 1) * HEAD_DIM)
        scores = lax.dot_general(
            q_ref[:, lanes], keys, (((1,), (1,)), ((), ())), preferred_element_type=f32
        ) * (1.0 / math.sqrt(HEAD_DIM))
        scores = jnp.where(allowed, scores, -1e30)
        weights = jnp.exp(scores - jnp.max(scores, axis=1, keepdims=True))
        shares = (weights / jnp.sum(weights, axis=1, keepdims=True)).astype(bf16)
        out_ref[:, lanes] = dot(shares, values).astype(bf16)


def attend(rows, lengths, q_at, k_at, v_at):
    width = Q_WIDTH // KV_HEADS
    return pl.pallas_call(
        attention_kernel,
        grid=(KV_HEADS,),
        in_specs=[
            scalars(),
            pl.BlockSpec((ROWS, width), lambda g: (0, q_at // width + g)),
            pl.BlockSpec((ROWS, HEAD_DIM), lambda g: (0, k_at // HEAD_DIM + g)),
            pl.BlockSpec((ROWS, HEAD_DIM), lambda g: (0, v_at // HEAD_DIM + g)),
        ],
        out_specs=pl.BlockSpec((ROWS, width), lambda g: (0, g)),
        out_shape=jax.ShapeDtypeStruct((ROWS, Q_WIDTH), bf16),
        compiler_params=BIG,
        cost_estimate=pl.CostEstimate(
            flops=4 * HEADS * ROWS * ROWS * HEAD_DIM, bytes_accessed=4 << 20, transcendentals=HEADS * ROWS * ROWS
        ),
    )(lengths, rows, rows, rows)


def advantage_kernel(place_ref, facts_ref, out_ref):
    coded = facts_ref[...].astype(f32)
    facts = coded + pltpu.roll(coded, 128 - 8, 1) + pltpu.roll(coded, 128 - 16, 1)
    row = lax.broadcasted_iota(jnp.int32, (ROWS, 128), 0)
    lane = lax.broadcasted_iota(jnp.int32, (ROWS, 128), 1)
    ids = pltpu.roll(facts, 128 - 2, 1)
    counted = (row % SPAN < 8) & (lane < 2)
    own = place_ref[0] * 4 + place_ref[1] * 2 + place_ref[2]
    other = place_ref[0] * 4 + place_ref[1] * 2 + 1 - place_ref[2]

    def fact(device, at):
        return jnp.sum(jnp.where((row == device * SPAN) & (lane == at), facts, 0.0))

    for j in range(4):
        device, mine = (own, other)[j // 2], j % 2
        reward, group = fact(device, mine), fact(device, 2 + mine)
        held = jnp.where(counted & (ids == group), facts, 0.0)
        center = jnp.sum(held, keepdims=True) / GROUP
        second = jnp.sum(held * held, keepdims=True) / GROUP
        spread = jnp.maximum(jnp.sqrt(jnp.maximum(second - center * center, 0.0)), std_floor)
        out_ref[j : j + 1, :] = jnp.broadcast_to((reward - center) / spread, (1, 128))
        out_ref[4 + j : 5 + j, :] = jnp.full((1, 128), fact(device, 4 + mine), f32)


def project_kernel(
    place_ref, own_p, other_p, own_r, other_r, target_ref,
    w0, sm, sp, s2p, s2e, o0, om, op, o2p, o2e,
    y_ref, stats_ref, rows_p, rows_r, weight_p, weight_r, sems,
):
    c, z, xh = place_ref[2], place_ref[3], place_ref[4]

    def load(source, first, weight, dz, side, sem):
        shard = lax.rem(z + 4 + dz, 4) * 2 + side
        at = pl.multiple_of(shard * SHARD, 64)
        return pltpu.make_async_copy(
            source.at[pl.ds(first, SHARD), :], weight.at[pl.ds(at, SHARD), :], sem
        )

    here, there = xh, 1 - xh
    copies_p = [
        pltpu.make_async_copy(own_p, rows_p.at[pl.ds(0, ROWS), :], sems.at[0]),
        pltpu.make_async_copy(other_p, rows_p.at[pl.ds(ROWS, ROWS), :], sems.at[0]),
    ]
    copies_r = [
        pltpu.make_async_copy(own_r, rows_r.at[pl.ds(0, ROWS), :], sems.at[1]),
        pltpu.make_async_copy(other_r, rows_r.at[pl.ds(ROWS, ROWS), :], sems.at[1]),
    ]
    for block, dz, side in ((w0, 0, here), (sm, -1, here), (sp, 1, here), (o0, 0, there), (om, -1, there), (op, 1, there)):
        copies_p.append(load(block, 0, weight_p, dz, side, sems.at[0]))
        copies_r.append(load(block, SHARD, weight_r, dz, side, sems.at[1]))
    for block, side in ((s2p, here), (o2p, there)):
        copies_p.append(load(block, 0, weight_p, 2, side, sems.at[0]))
    for block, side in ((s2e, here), (o2e, there)):
        copies_r.append(load(block, 0, weight_r, 2, side, sems.at[1]))
    for copy in copies_p + copies_r:
        copy.start()

    def lanes_of(value):
        total = value[:, :128]
        for k in range(1, value.shape[1] // 128):
            total = total + value[:, k * 128 : (k + 1) * 128]
        return total

    def run(rows, weight, keep):
        def step(j, sums):
            squares, products = sums
            at = pl.multiple_of(j * CHUNK, CHUNK)
            y = dot(rows[...], weight[:, pl.ds(at, CHUNK)])
            if keep:
                y_ref[:, pl.ds(at, CHUNK)] = y
            mine = target_ref[:, pl.ds(pl.multiple_of(c * HALF + at, 128), CHUNK)]
            theirs = target_ref[:, pl.ds(pl.multiple_of((1 - c) * HALF + at, 128), CHUNK)]
            target = jnp.concatenate([mine, theirs], axis=0).astype(f32)
            return squares + lanes_of(y * y), products + lanes_of(y * target)

        zero = jnp.zeros((2 * ROWS, 128), f32)
        squares, products = lax.fori_loop(0, HALF // CHUNK, step, (zero, zero))
        return jnp.sum(squares, axis=1, keepdims=True), jnp.sum(products, axis=1, keepdims=True)

    for copy in copies_p:
        copy.wait()
    policy_squares, policy_products = run(rows_p, weight_p, True)
    for copy in copies_r:
        copy.wait()
    reference_squares, reference_products = run(rows_r, weight_r, False)
    lane = lax.broadcasted_iota(jnp.int32, (2 * ROWS, 128), 1)
    stats_ref[...] = jnp.where(
        lane == 0,
        policy_squares,
        jnp.where(lane == 1, policy_products, jnp.where(lane == 2, reference_squares, reference_products)),
    )


def project(place, outs, target, weights):
    return pl.pallas_call(
        project_kernel,
        in_specs=[scalars()]
        + [in_place()] * 4
        + [pl.BlockSpec((ROWS, D_OUT), lambda i: (0, 0))]
        + [in_place()] * len(weights),
        grid=(1,),
        out_specs=[
            pl.BlockSpec((2 * ROWS, HALF), lambda i: (0, 0)),
            pl.BlockSpec((2 * ROWS, 128), lambda i: (0, 0)),
        ],
        out_shape=[
            jax.ShapeDtypeStruct((2 * ROWS, HALF), f32),
            jax.ShapeDtypeStruct((2 * ROWS, 128), f32),
        ],
        scratch_shapes=[
            VMEM((2 * ROWS, Q_WIDTH), bf16),
            VMEM((2 * ROWS, Q_WIDTH), bf16),
            VMEM((Q_WIDTH, HALF), bf16),
            VMEM((Q_WIDTH, HALF), bf16),
            pltpu.SemaphoreType.DMA((2,)),
        ],
        compiler_params=BIG,
        cost_estimate=pl.CostEstimate(
            flops=8 * ROWS * Q_WIDTH * HALF, bytes_accessed=24 << 20, transcendentals=0
        ),
    )(place, *outs, target, *weights)


def gradient_kernel(
    place_ref, own_ref, other_ref, y_ref, stats_ref, more_ref, target_ref, facts_ref,
    a0, a1, a2, a3, b0, b1, b2, b3, rows, grad, terms,
):
    y_at, c, z = place_ref[0], place_ref[2], place_ref[3]
    rows[:ROWS, :] = own_ref[...]
    rows[ROWS:, :] = other_ref[...]
    row = lax.broadcasted_iota(jnp.int32, (ROWS, 1), 0)
    for side in range(2):
        here = slice(side * ROWS, (side + 1) * ROWS)
        there = slice((1 - side) * ROWS, (2 - side) * ROWS)
        stats = stats_ref[here, :] + more_ref[there, :]
        policy_squares, policy_products = stats[:, 0:1], stats[:, 1:2]
        reference_squares, reference_products = stats[:, 2:3], stats[:, 3:4]
        one, two = 2 * side, 2 * side + 1
        early = row.astype(f32) < facts_ref[4 + one : 5 + one, 0:1]
        length = jnp.where(early, facts_ref[4 + one : 5 + one, 0:1], facts_ref[4 + two : 5 + two, 0:1])
        advantage = jnp.where(early, facts_ref[one : one + 1, 0:1], facts_ref[two : two + 1, 0:1])
        policy_norm = jnp.sqrt(policy_squares / D_OUT + norm_epsilon)
        reference_norm = jnp.sqrt(reference_squares / D_OUT + norm_epsilon)
        policy_self = policy_squares / (policy_norm * policy_norm)
        policy_cross = policy_products / policy_norm
        reference_self = reference_squares / (reference_norm * reference_norm)
        reference_cross = reference_products / reference_norm
        gain = ((policy_self - reference_self) - 2.0 * (policy_cross - reference_cross)) * (
            1.0 / (4.0 * math.sqrt(D_OUT))
        )
        weight = (advantage - kl_weight * (1.0 - jnp.exp(gain))) / length
        along = (policy_self - policy_cross) / D_OUT
        scale = weight / policy_norm
        slope = scale * (1.0 - along) / policy_norm
        side_lanes = c if side == 0 else 1 - c
        target = target_ref[:, pl.ds(pl.multiple_of(side_lanes * HALF, 128), HALF)].astype(f32)
        grad[here, :] = (y_ref[here, :] * slope - target * scale).astype(bf16)

    def term(first, lanes):
        return lax.dot_general(
            rows[:, pl.ds(first, PIECE)], grad[:, lanes], (((0,), (0,)), ((), ())), preferred_element_type=f32
        ).astype(bf16)

    for d, out in enumerate((a0, a1, a2, a3)):
        out[...] = term(pl.multiple_of(lax.rem(z + d, 4) * PIECE, 128), slice(0, PIECE))
    for k in range(4):
        terms[...] = term(k * PIECE, slice(PIECE, HALF)).reshape(2, 4, 80, PIECE)
        for d, out in enumerate((b0, b1, b2, b3)):
            out[2 * k : 2 * k + 2] = terms[:, lax.rem(y_at + d, 4)]


def gradient(place, own, other, y, stats, more, target, facts):
    block = lambda *shape: pl.BlockSpec(shape, lambda i: (0,) * len(shape))
    return pl.pallas_call(
        gradient_kernel,
        grid=(1,),
        in_specs=[
            scalars(),
            block(ROWS, Q_WIDTH),
            block(ROWS, Q_WIDTH),
            block(2 * ROWS, HALF),
            block(2 * ROWS, 128),
            block(2 * ROWS, 128),
            block(ROWS, D_OUT),
            block(8, 128),
        ],
        out_specs=[block(PIECE, PIECE)] * 4 + [block(8, 80, PIECE)] * 4,
        out_shape=[jax.ShapeDtypeStruct((PIECE, PIECE), bf16)] * 4
        + [jax.ShapeDtypeStruct((8, 80, PIECE), bf16)] * 4,
        scratch_shapes=[
            VMEM((2 * ROWS, Q_WIDTH), bf16),
            VMEM((2 * ROWS, HALF), bf16),
            VMEM((2, 4, 80, PIECE), bf16),
        ],
        compiler_params=BIG,
        cost_estimate=pl.CostEstimate(
            flops=4 * ROWS * Q_WIDTH * HALF, bytes_accessed=16 << 20, transcendentals=0
        ),
    )(place, own, other, y, stats, more, target, facts)


def total_of(refs, index):
    total = refs[0][index].astype(f32)
    for ref in refs[1:]:
        total = total + ref[index].astype(f32)
    return total


def sum_kernel(axis, place_at, place_ref, *refs):
    parts, outs = refs[:4], refs[4:]
    own = place_ref[place_at]
    for d, out in enumerate(outs):
        at = lax.rem(own + d, 4)
        index = (slice(None), at) if axis == 1 else (at,)
        out[...] = total_of(parts, index).astype(bf16)


def sum_blocks(place, parts, axis, place_at):
    shape = (2, 80, PIECE)
    return pl.pallas_call(
        functools.partial(sum_kernel, axis, place_at),
        in_specs=[scalars()] + [whole()] * 4,
        out_specs=[whole()] * 4,
        out_shape=[jax.ShapeDtypeStruct(shape, bf16)] * 4,
        compiler_params=BIG,
        cost_estimate=pl.CostEstimate(flops=4 << 20, bytes_accessed=5 << 20, transcendentals=0),
    )(place, *parts)


def last_sum_kernel(place_ref, *refs):
    first, second, keep, send = refs[:4], refs[4:8], refs[8], refs[9]
    xh = place_ref[4]
    for out, at in ((keep, xh), (send, 1 - xh)):
        out[:, :PIECE] = total_of(first, (at,)).astype(bf16)
        out[:, PIECE:] = total_of(second, (at,)).astype(bf16)


def last_sum(place, first, second):
    return pl.pallas_call(
        last_sum_kernel,
        in_specs=[scalars()] + [whole()] * 8,
        out_specs=[whole()] * 2,
        out_shape=[jax.ShapeDtypeStruct((80, HALF), bf16)] * 2,
        compiler_params=BIG,
    )(place, *first, *second)


def step_kernel(
    place_ref, square_ref, mine_ref, theirs_ref, weight_ref, ema_ref, update_ref, moved_ref, next_ref
):
    scale = lax.rsqrt(square_ref[0:1, 0:1] / (Q_WIDTH * D_OUT) + norm_epsilon)
    c = place_ref[2]
    for half in range(2):
        lanes = slice(half * HALF, (half + 1) * HALF)
        grad = jnp.where(c == half, mine_ref[0].astype(f32), theirs_ref[0].astype(f32))
        update = grad * scale
        moved = weight_ref[:, lanes].astype(f32) - step_size * update
        update_ref[:, lanes] = update
        moved_ref[:, lanes] = moved.astype(bf16)
        next_ref[:, lanes] = ema_decay * ema_ref[:, lanes] + (1.0 - ema_decay) * moved


def take_step(place, square_sum, mine, theirs, policy_weight, ema_weight):
    wide = lambda: pl.BlockSpec((80, D_OUT), lambda i, place: (i, 0))
    turned = lambda: pl.BlockSpec((1, 80, HALF), lambda i, place: (lax.rem(i + 4 - place[0], 4), 0, 0))
    return pl.pallas_call(
        step_kernel,
        grid_spec=pltpu.PrefetchScalarGridSpec(
            num_scalar_prefetch=1,
            grid=(4,),
            in_specs=[pl.BlockSpec((8, 128), lambda i, place: (0, 0)), turned(), turned(), wide(), wide()],
            out_specs=[wide()] * 3,
        ),
        out_shape=[
            jax.ShapeDtypeStruct((SHARD, D_OUT), f32),
            jax.ShapeDtypeStruct((SHARD, D_OUT), bf16),
            jax.ShapeDtypeStruct((SHARD, D_OUT), f32),
        ],
        compiler_params=BIG,
    )(place, square_sum, mine, theirs, policy_weight, ema_weight)


def local(
    q_policy,
    kv_policy,
    q_reference,
    kv_reference,
    target,
    send_slot,
    lengths,
    rewards,
    group_ids,
    policy_weight,
    ema_weight,
):
    place = jnp.stack([lax.axis_index(name) for name in EVERY]).astype(jnp.int32)
    c = place[2]
    send = lax.ppermute

    def half(weight):
        return lax.dynamic_slice_in_dim(weight, c * HALF, HALF, 1).astype(bf16)

    w0 = jnp.concatenate([half(policy_weight), half(ema_weight)], axis=0)
    sm = send(w0, "z", ring(1))
    sp = send(w0, "z", ring(-1))
    o0 = send(w0, ("xl", "xh"), ACROSS)

    facts = jnp.concatenate(
        [rewards, group_ids.astype(f32), lengths[0].astype(f32), jnp.zeros((2,), f32)]
    )[None, :]
    facts = jnp.concatenate([facts, send(facts, "xh", FLIP)], axis=0)
    facts = jnp.concatenate([facts] + [send(facts, "z", ring(d)) for d in (1, 2, 3)], axis=0)
    facts = jnp.pad(jnp.tile(facts, (2, 3)), ((0, 0), (0, 128 - 24)))

    rows_policy = pl.pallas_call(
        pack_policy_kernel,
        in_specs=[whole()] * 3,
        out_specs=whole(),
        out_shape=jax.ShapeDtypeStruct((ROWS, Q_WIDTH + 1024), bf16),
        compiler_params=BIG,
    )(send_slot, q_policy, kv_policy)
    rows_policy = lax.all_to_all(rows_policy, DP, split_axis=0, concat_axis=0, tiled=True)

    s2p = send(sm[:SHARD], "z", ring(1))
    s2e = send(sp[SHARD:], "z", ring(-1))
    om = send(sm, ("xl", "xh"), ACROSS)
    op = send(o0, "z", ring(-1))

    rows_reference = pl.pallas_call(
        pack_reference_kernel,
        in_specs=[whole()] * 5,
        out_specs=whole(),
        out_shape=jax.ShapeDtypeStruct((ROWS, D_OUT + Q_WIDTH + 1024 + 128), bf16),
        compiler_params=BIG,
    )(send_slot, q_reference, kv_reference, target, facts)
    rows_reference = lax.all_to_all(rows_reference, DP, split_axis=0, concat_axis=0, tiled=True)

    out_policy = attend(rows_policy, lengths, 0, Q_WIDTH, Q_WIDTH + 512)
    other_policy = send(out_policy, "c", FLIP)

    o2p = send(s2p, ("xl", "xh"), ACROSS)
    o2e = send(om[SHARD:], "z", ring(1))

    out_reference = attend(rows_reference, lengths, D_OUT, D_OUT + Q_WIDTH, D_OUT + Q_WIDTH + 512)
    other_reference = send(out_reference, "c", FLIP)
    advantages = pl.pallas_call(
        advantage_kernel,
        grid=(1,),
        in_specs=[scalars(), pl.BlockSpec((ROWS, 128), lambda i: (0, (D_OUT + Q_WIDTH + 1024) // 128))],
        out_specs=pl.BlockSpec((8, 128), lambda i: (0, 0)),
        out_shape=jax.ShapeDtypeStruct((8, 128), f32),
        compiler_params=BIG,
    )(place, rows_reference)

    y_policy, stats = project(
        place,
        (out_policy, other_policy, out_reference, other_reference),
        rows_reference,
        (w0, sm, sp, s2p, s2e, o0, om, op, o2p, o2e),
    )
    more = send(stats, "c", FLIP)
    pieces = gradient(place, out_policy, other_policy, y_policy, stats, more, rows_reference, advantages)

    first, second = pieces[:4], pieces[4:]
    first = [first[0]] + [send(first[d], "z", ring(d)) for d in (1, 2, 3)]
    second = [second[0]] + [send(second[d], "y", ring(d)) for d in (1, 2, 3)]
    first = sum_blocks(place, [piece.reshape(2, 4, 80, PIECE) for piece in first], 1, 0)
    second = sum_blocks(place, [piece.reshape(4, 2, 80, PIECE) for piece in second], 0, 3)
    first = [first[0]] + [send(first[d], "y", ring(d)) for d in (1, 2, 3)]
    second = [second[0]] + [send(second[d], "z", ring(d)) for d in (1, 2, 3)]
    kept, given = last_sum(place, first, second)

    def add(one, two):
        return (one.astype(f32) + two.astype(f32)).astype(bf16)

    block = add(kept, send(given, ("xl", "xh"), ACROSS))
    block = add(block, send(block, "xl", FLIP))

    mine = jnp.stack([block] + [send(block, "y", ring(-d)) for d in (1, 2, 3)])
    theirs = send(mine, "c", FLIP)
    square = jnp.sum(jnp.square(mine.astype(f32)), axis=(1, 2)) + jnp.sum(
        jnp.square(theirs.astype(f32)), axis=(1, 2)
    )
    square = (square[0] + square[2]) + (square[1] + square[3])
    square = jnp.broadcast_to(square, (8, 128))
    square = square + send(square, ("xl", "xh"), ACROSS)
    square = (square + send(square, "z", ring(2))) + (send(square, "z", ring(1)) + send(square, "z", ring(3)))
    return tuple(take_step(place, square, mine, theirs, policy_weight, ema_weight))


def solution(mesh):
    names = Mesh(mesh.devices.reshape(4, 2, 2, 4, 2), EVERY)
    rows, whole_rows = P(EVERY, None), P(EVERY)
    in_specs = (rows,) * 7 + (whole_rows,) * 2 + (P(FSDP, None),) * 2
    out_specs = (P(FSDP, None),) * 3
    return jax.shard_map(local, mesh=names, in_specs=in_specs, out_specs=out_specs, check_vma=False)
```

```python
import functools
import math

import jax
import jax.numpy as jnp
from jax import lax
from jax.experimental import pallas as pl
from jax.experimental.pallas import tpu as pltpu
from jax.sharding import Mesh
from jax.sharding import PartitionSpec as P

HEADS = 20
KV_HEADS = 4
HEAD_DIM = 128
D_OUT = 2560
GROUP = 8
Q_WIDTH = 2560
ROWS = 256
SPAN = 16
SHARD = 320
HALF = 1280
CHUNK = 256
PIECE = 640
LATE = 384
TARGET_AT = 3584
FACTS_AT = 6144

kl_weight = 0.1
step_size = 0.02
ema_decay = 0.95
std_floor = 0.6
norm_epsilon = 1e-06

bf16 = jnp.bfloat16
f32 = jnp.float32
VMEM = pltpu.VMEM
SMEM = pltpu.SMEM
BIG = pltpu.CompilerParams(vmem_limit_bytes=56 * 1024 * 1024)
SMALL = pltpu.CompilerParams(vmem_limit_bytes=24 * 1024 * 1024)

DP = ("y", "xl", "c")
FSDP = ("z", "xh")
EVERY = DP + FSDP


def ring(step):
    return [(i, (i + step) % 4) for i in range(4)]


FLIP = [(0, 1), (1, 0)]
ACROSS = [(2, 1), (1, 2), (0, 3), (3, 0)]


def whole(shape=None):
    return pl.BlockSpec(memory_space=VMEM)


def scalars():
    return pl.BlockSpec(memory_space=SMEM)


def in_place():
    return pl.BlockSpec(memory_space=pl.ANY)


def dot(a, b):
    return jnp.dot(a, b, preferred_element_type=f32)


def one_hot_rows(slots_ref):
    return (lax.broadcasted_iota(jnp.int32, (ROWS, ROWS), 0) == slots_ref[...]).astype(bf16)


def pack_rows_kernel(slots_ref, q_ref, kv_ref, *rest):
    out_ref = rest[-1]
    pick = one_hot_rows(slots_ref)
    out_ref[:, :Q_WIDTH] = dot(pick, q_ref[...]).astype(bf16)
    out_ref[:, Q_WIDTH : Q_WIDTH + 1024] = dot(pick, kv_ref[...]).astype(bf16)


def pack_policy_kernel(rewards_ref, ids_ref, lengths_ref, slots_ref, q_ref, kv_ref, target_ref, *rest):
    out_ref = rest[-1]
    pack_rows_kernel(slots_ref, q_ref, kv_ref, out_ref)
    rows = dot(one_hot_rows(slots_ref), target_ref[...]).astype(bf16)
    left, right = slice(TARGET_AT, TARGET_AT + HALF), slice(TARGET_AT + HALF, TARGET_AT + D_OUT)
    for pair in range(ROWS // (2 * SPAN)):
        top = pair * 2 * SPAN
        one, two = slice(top, top + SPAN), slice(top + SPAN, top + 2 * SPAN)
        out_ref[one, left] = rows[one, :HALF]
        out_ref[one, right] = rows[two, :HALF]
        out_ref[two, left] = rows[one, HALF:]
        out_ref[two, right] = rows[two, HALF:]
    lane = lax.broadcasted_iota(jnp.int32, (8, 128), 1)
    facts = jnp.zeros((8, 128), f32)
    given = (rewards_ref[0], rewards_ref[1], ids_ref[0], ids_ref[1], lengths_ref[0, 0], lengths_ref[0, 1])
    for k, fact in enumerate(given):
        facts = jnp.where(lane % 8 == k, fact.astype(f32), facts)
    high = facts.astype(bf16).astype(f32)
    middle = (facts - high).astype(bf16).astype(f32)
    low = facts - high - middle
    coded = jnp.where(lane < 8, high, jnp.where(lane < 16, middle, low))
    out_ref[:, FACTS_AT:] = jnp.broadcast_to(coded[0:1], (ROWS, 128)).astype(bf16)


def pack(kernel, width, operands, after=(), small=()):
    return pl.pallas_call(
        kernel,
        in_specs=[scalars()] * len(small) + [whole()] * len(operands) + [in_place()] * len(after),
        out_specs=whole(),
        out_shape=jax.ShapeDtypeStruct((ROWS, width), bf16),
        compiler_params=BIG,
        cost_estimate=pl.CostEstimate(
            flops=2 * ROWS * ROWS * width, bytes_accessed=4 * ROWS * width, transcendentals=0
        ),
    )(*small, *operands, *after)


def attention_kernel(lengths_ref, q_ref, k_ref, v_ref, *rest):
    out_ref = rest[-1]
    row = lax.broadcasted_iota(jnp.int32, (ROWS, ROWS), 0)
    column = lax.broadcasted_iota(jnp.int32, (ROWS, ROWS), 1)
    bound = lengths_ref[0, 0]
    allowed = (column <= row) & ((column >= bound) | (row < bound))
    keys, values = k_ref[...], v_ref[...]
    for head in range(HEADS // KV_HEADS):
        lanes = slice(head * HEAD_DIM, (head + 1) * HEAD_DIM)
        scores = lax.dot_general(
            q_ref[:, lanes], keys, (((1,), (1,)), ((), ())), preferred_element_type=f32
        ) * (1.0 / math.sqrt(HEAD_DIM))
        scores = jnp.where(allowed, scores, -1e30)
        weights = jnp.exp(scores - jnp.max(scores, axis=1, keepdims=True))
        shares = (weights / jnp.sum(weights, axis=1, keepdims=True)).astype(bf16)
        out_ref[:, lanes] = dot(shares, values).astype(bf16)


def attend(rows, lengths, after):
    q_at, k_at, v_at = 0, Q_WIDTH, Q_WIDTH + 512
    width = Q_WIDTH // KV_HEADS
    return pl.pallas_call(
        attention_kernel,
        grid=(KV_HEADS,),
        in_specs=[
            scalars(),
            pl.BlockSpec((ROWS, width), lambda g: (0, q_at // width + g)),
            pl.BlockSpec((ROWS, HEAD_DIM), lambda g: (0, k_at // HEAD_DIM + g)),
            pl.BlockSpec((ROWS, HEAD_DIM), lambda g: (0, v_at // HEAD_DIM + g)),
        ]
        + [in_place()] * len(after),
        out_specs=pl.BlockSpec((ROWS, width), lambda g: (0, g)),
        out_shape=jax.ShapeDtypeStruct((ROWS, Q_WIDTH), bf16),
        compiler_params=BIG,
        cost_estimate=pl.CostEstimate(
            flops=4 * HEADS * ROWS * ROWS * HEAD_DIM, bytes_accessed=4 << 20, transcendentals=HEADS * ROWS * ROWS
        ),
    )(lengths, rows, rows, rows, *after)


def facts_kernel(coded_ref, out_ref):
    for block in range(ROWS // SPAN):
        coded = coded_ref[block * SPAN : (block + 1) * SPAN, :].astype(f32)[:8]
        facts = coded + pltpu.roll(coded, 128 - 8, 1) + pltpu.roll(coded, 128 - 16, 1)
        out_ref[block : block + 1, :] = facts[0:1]


def advantage_kernel(place_ref, facts_ref, out_ref):
    facts = facts_ref[...]
    row = lax.broadcasted_iota(jnp.int32, facts.shape, 0)
    lane = lax.broadcasted_iota(jnp.int32, facts.shape, 1)
    ids = pltpu.roll(facts, 128 - 2, 1)
    own = place_ref[0] * 4 + place_ref[1] * 2 + place_ref[2]
    other = place_ref[0] * 4 + place_ref[1] * 2 + 1 - place_ref[2]

    def fact(device, at):
        return jnp.sum(jnp.where((row == device) & (lane == at), facts, 0.0))

    for j in range(4):
        device, mine = (own, other)[j // 2], j % 2
        reward, group = fact(device, mine), fact(device, 2 + mine)
        held = jnp.where((lane < 2) & (ids == group), facts, 0.0)
        center = jnp.sum(held, keepdims=True) / GROUP
        second = jnp.sum(held * held, keepdims=True) / GROUP
        spread = jnp.maximum(jnp.sqrt(jnp.maximum(second - center * center, 0.0)), std_floor)
        out_ref[j : j + 1, :] = jnp.broadcast_to((reward - center) / spread, (1, 128))
        out_ref[4 + j : 5 + j, :] = jnp.full((1, 128), fact(device, 4 + mine), f32)


def project_most_kernel(
    place_ref, own_p, other_p, own_r, other_r,
    p0, spp, o0p, smp, s2p, omp, e0, spe, o0e, sme, s2e, ome,
    y_p, y_r, late_p, late_r, rows_p, rows_r, weight_p, weight_r, sems,
):
    z, xh = place_ref[3], place_ref[4]

    def place_of(dz, side):
        return pl.multiple_of((lax.rem(z + 4 + dz, 4) * 2 + side) * SHARD, 64)

    here, there = xh, 1 - xh
    copies = []
    for own, other, rows, weight, blocks, sem in (
        (own_p, other_p, rows_p, weight_p, (p0, smp, spp, o0p, s2p, omp), sems.at[0]),
        (own_r, other_r, rows_r, weight_r, (e0, sme, spe, o0e, s2e, ome), sems.at[1]),
    ):
        group = [
            pltpu.make_async_copy(own, rows.at[pl.ds(0, ROWS), :], sem),
            pltpu.make_async_copy(other, rows.at[pl.ds(ROWS, ROWS), :], sem),
        ]
        for block, dz, side in zip(blocks, (0, -1, 1, 0, 2, -1), (here, here, here, there, here, there)):
            group.append(pltpu.make_async_copy(block, weight.at[pl.ds(place_of(dz, side), SHARD), :], sem))
        for copy in group:
            copy.start()
        copies.append(group)
    for weight in (weight_p, weight_r):
        for dz in (1, 2):
            weight[pl.ds(place_of(dz, there), SHARD), :] = jnp.zeros((SHARD, HALF), bf16)

    def run(rows, weight, out, late):
        def step(j, carry):
            at = pl.multiple_of(j * CHUNK, CHUNK)
            out[:, pl.ds(at, CHUNK)] = dot(rows[...], weight[:, pl.ds(at, CHUNK)])
            return carry

        lax.fori_loop(0, HALF // CHUNK, step, 0)
        for k, dz in enumerate((1, 2)):
            at = pl.multiple_of(lax.rem(z + dz, 4) * PIECE, 128)
            part = rows[:, pl.ds(at, PIECE)].astype(f32)
            part = jnp.where(there == 0, part, pltpu.roll(part, PIECE - SHARD, 1))
            late[:, k * LATE : (k + 1) * LATE] = part[:, :LATE].astype(bf16)

    for copy in copies[0]:
        copy.wait()
    run(rows_p, weight_p, y_p, late_p)
    for copy in copies[1]:
        copy.wait()
    run(rows_r, weight_r, y_r, late_r)


def project_most(place, outs, weights):
    return pl.pallas_call(
        project_most_kernel,
        in_specs=[scalars()] + [in_place()] * (len(outs) + len(weights)),
        out_specs=[whole()] * 4,
        out_shape=[jax.ShapeDtypeStruct((2 * ROWS, HALF), f32)] * 2
        + [jax.ShapeDtypeStruct((2 * ROWS, 2 * LATE), bf16)] * 2,
        scratch_shapes=[
            VMEM((2 * ROWS, Q_WIDTH), bf16),
            VMEM((2 * ROWS, Q_WIDTH), bf16),
            VMEM((Q_WIDTH, HALF), bf16),
            VMEM((Q_WIDTH, HALF), bf16),
            pltpu.SemaphoreType.DMA((2,)),
        ],
        compiler_params=BIG,
        cost_estimate=pl.CostEstimate(
            flops=8 * ROWS * Q_WIDTH * HALF, bytes_accessed=24 << 20, transcendentals=0
        ),
    )(place, *outs, *weights)


def project_last_kernel(
    place_ref, rows_p, rows_r, opp, o2p, ope, o2e, y_p, y_r, mine_ref, theirs_ref,
    y_ref, stats_ref, late_p, late_r, sums,
):
    j = pl.program_id(0)

    @pl.when(j == 0)
    def _():
        sums[...] = jnp.zeros_like(sums)
        for late in (late_p, late_r):
            late[SHARD:LATE, :] = jnp.zeros((LATE - SHARD, CHUNK), bf16)
            late[LATE + SHARD :, :] = jnp.zeros((LATE - SHARD, CHUNK), bf16)

    for late, first, second in ((late_p, opp, o2p), (late_r, ope, o2e)):
        late[:SHARD, :] = first[...]
        late[LATE : LATE + SHARD, :] = second[...]

    def lanes_of(value):
        return value[:, :128] + value[:, 128:]

    target = jnp.concatenate([mine_ref[...], theirs_ref[...]], axis=0).astype(f32)
    y = y_p[...] + dot(rows_p[...], late_p[...])
    y_ref[...] = y
    sums[0] += lanes_of(y * y)
    sums[1] += lanes_of(y * target)
    y = y_r[...] + dot(rows_r[...], late_r[...])
    sums[2] += lanes_of(y * y)
    sums[3] += lanes_of(y * target)

    @pl.when(j == HALF // CHUNK - 1)
    def _():
        lane = lax.broadcasted_iota(jnp.int32, (2 * ROWS, 128), 1)
        stats = jnp.zeros((2 * ROWS, 128), f32)
        for k in range(4):
            stats = jnp.where(lane == k, jnp.sum(sums[k], axis=1, keepdims=True), stats)
        stats_ref[...] = stats


def project_last(place, parts, weights, target):
    steps = HALF // CHUNK
    chunk = lambda rows: pl.BlockSpec((rows, CHUNK), lambda j, place: (0, j))
    fixed = lambda width: pl.BlockSpec((2 * ROWS, width), lambda j, place: (0, 0))
    y_p, y_r, rows_p, rows_r = parts
    return pl.pallas_call(
        project_last_kernel,
        grid_spec=pltpu.PrefetchScalarGridSpec(
            num_scalar_prefetch=1,
            grid=(steps,),
            in_specs=[fixed(2 * LATE)] * 2
            + [chunk(SHARD)] * 4
            + [chunk(2 * ROWS)] * 2
            + [
                pl.BlockSpec((ROWS, CHUNK), lambda j, place: (0, TARGET_AT // CHUNK + place[2] * steps + j)),
                pl.BlockSpec((ROWS, CHUNK), lambda j, place: (0, TARGET_AT // CHUNK + (1 - place[2]) * steps + j)),
            ],
            out_specs=[chunk(2 * ROWS), fixed(128)],
            scratch_shapes=[
                VMEM((2 * LATE, CHUNK), bf16),
                VMEM((2 * LATE, CHUNK), bf16),
                VMEM((4, 2 * ROWS, 128), f32),
            ],
        ),
        out_shape=[
            jax.ShapeDtypeStruct((2 * ROWS, HALF), f32),
            jax.ShapeDtypeStruct((2 * ROWS, 128), f32),
        ],
        compiler_params=BIG,
        cost_estimate=pl.CostEstimate(
            flops=2 * ROWS * Q_WIDTH * HALF, bytes_accessed=10 << 20, transcendentals=0
        ),
    )(place, rows_p, rows_r, *weights, y_p, y_r, target, target)


def gradient_kernel(
    place_ref, own_ref, other_ref, y_ref, stats_ref, more_ref, target_ref, facts_ref,
    a0, a1, a2, a3, grad, rows,
):
    c, z = place_ref[2], place_ref[3]
    rows[:ROWS, :] = own_ref[...]
    rows[ROWS:, :] = other_ref[...]
    row = lax.broadcasted_iota(jnp.int32, (ROWS, 1), 0)
    for side in range(2):
        here = slice(side * ROWS, (side + 1) * ROWS)
        there = slice((1 - side) * ROWS, (2 - side) * ROWS)
        stats = stats_ref[here, :] + more_ref[there, :]
        policy_squares, policy_products = stats[:, 0:1], stats[:, 1:2]
        reference_squares, reference_products = stats[:, 2:3], stats[:, 3:4]
        one, two = 2 * side, 2 * side + 1
        early = row.astype(f32) < facts_ref[4 + one : 5 + one, 0:1]
        length = jnp.where(early, facts_ref[4 + one : 5 + one, 0:1], facts_ref[4 + two : 5 + two, 0:1])
        advantage = jnp.where(early, facts_ref[one : one + 1, 0:1], facts_ref[two : two + 1, 0:1])
        policy_norm = jnp.sqrt(policy_squares / D_OUT + norm_epsilon)
        reference_norm = jnp.sqrt(reference_squares / D_OUT + norm_epsilon)
        policy_self = policy_squares / (policy_norm * policy_norm)
        policy_cross = policy_products / policy_norm
        reference_self = reference_squares / (reference_norm * reference_norm)
        reference_cross = reference_products / reference_norm
        gain = ((policy_self - reference_self) - 2.0 * (policy_cross - reference_cross)) * (
            1.0 / (4.0 * math.sqrt(D_OUT))
        )
        weight = (advantage - kl_weight * (1.0 - jnp.exp(gain))) / length
        along = (policy_self - policy_cross) / D_OUT
        scale = weight / policy_norm
        slope = scale * (1.0 - along) / policy_norm
        side_lanes = c if side == 0 else 1 - c
        target = target_ref[:, pl.ds(pl.multiple_of(TARGET_AT + side_lanes * HALF, 128), HALF)].astype(f32)
        grad[here, :] = (y_ref[here, :] * slope - target * scale).astype(bf16)

    for d, out in enumerate((a0, a1, a2, a3)):
        first = pl.multiple_of(lax.rem(z + d, 4) * PIECE, 128)
        out[...] = outer(rows[:, pl.ds(first, PIECE)], grad[:, :PIECE])


def outer(rows, grad):
    return lax.dot_general(rows, grad, (((0,), (0,)), ((), ())), preferred_element_type=f32).astype(bf16)


def second_half_kernel(place_ref, own_ref, other_ref, grad_ref, b0, b1, b2, b3, rows, terms):
    rows[:ROWS, :] = own_ref[...]
    rows[ROWS:, :] = other_ref[...]
    for k in range(4):
        terms[...] = outer(rows[:, k * PIECE : (k + 1) * PIECE], grad_ref[:, PIECE:]).reshape(2, 4, 80, PIECE)
        for d, out in enumerate((b0, b1, b2, b3)):
            out[2 * k : 2 * k + 2] = terms[:, lax.rem(place_ref[0] + d, 4)]


def gradient(place, own, other, y, stats, more, target, facts):
    cost = pl.CostEstimate(flops=2 * ROWS * Q_WIDTH * HALF, bytes_accessed=8 << 20, transcendentals=0)
    *first, grad = pl.pallas_call(
        gradient_kernel,
        in_specs=[scalars()] + [whole()] * 7,
        out_specs=[whole()] * 5,
        out_shape=[jax.ShapeDtypeStruct((PIECE, PIECE), bf16)] * 4
        + [jax.ShapeDtypeStruct((2 * ROWS, HALF), bf16)],
        scratch_shapes=[VMEM((2 * ROWS, Q_WIDTH), bf16)],
        compiler_params=SMALL,
        cost_estimate=cost,
    )(place, own, other, y, stats, more, target, facts)
    second = pl.pallas_call(
        second_half_kernel,
        in_specs=[scalars()] + [whole()] * 3,
        out_specs=[whole()] * 4,
        out_shape=[jax.ShapeDtypeStruct((8, 80, PIECE), bf16)] * 4,
        scratch_shapes=[VMEM((2 * ROWS, Q_WIDTH), bf16), VMEM((2, 4, 80, PIECE), bf16)],
        compiler_params=SMALL,
        cost_estimate=cost,
    )(place, own, other, grad)
    return first, second


def total_of(refs, index):
    total = refs[0][index].astype(f32)
    for ref in refs[1:]:
        total = total + ref[index].astype(f32)
    return total


def sum_kernel(axis, place_at, place_ref, *refs):
    parts, outs = refs[:4], refs[4:]
    own = place_ref[place_at]
    for d, out in enumerate(outs):
        at = lax.rem(own + d, 4)
        index = (slice(None), at) if axis == 1 else (at,)
        out[...] = total_of(parts, index).astype(bf16)


def sum_blocks(place, parts, axis, place_at):
    shape = (2, 80, PIECE)
    return pl.pallas_call(
        functools.partial(sum_kernel, axis, place_at),
        in_specs=[scalars()] + [whole()] * 4,
        out_specs=[whole()] * 4,
        out_shape=[jax.ShapeDtypeStruct(shape, bf16)] * 4,
        compiler_params=SMALL,
        cost_estimate=pl.CostEstimate(flops=4 << 20, bytes_accessed=5 << 20, transcendentals=0),
    )(place, *parts)


def last_sum_kernel(place_ref, *refs):
    first, second, keep, send = refs[:4], refs[4:8], refs[8], refs[9]
    xh = place_ref[4]
    for out, at in ((keep, xh), (send, 1 - xh)):
        out[:, :PIECE] = total_of(first, (at,)).astype(bf16)
        out[:, PIECE:] = total_of(second, (at,)).astype(bf16)


def last_sum(place, first, second):
    return pl.pallas_call(
        last_sum_kernel,
        in_specs=[scalars()] + [whole()] * 8,
        out_specs=[whole()] * 2,
        out_shape=[jax.ShapeDtypeStruct((80, HALF), bf16)] * 2,
        compiler_params=SMALL,
    )(place, *first, *second)


def step_kernel(
    place_ref, square_ref, mine_ref, theirs_ref, weight_ref, ema_ref,
    update_out, moved_out, next_out, update, moved, after, sems,
):
    scale = lax.rsqrt(square_ref[0:1, 0:1] / (Q_WIDTH * D_OUT) + norm_epsilon)
    y_at, c = place_ref[0], place_ref[2]
    copies = []
    for d in range(4):
        rows = pl.ds(pl.multiple_of(lax.rem(y_at + d, 4) * 80, 16), 80)
        for side, grad_ref in ((c, mine_ref), (1 - c, theirs_ref)):
            lanes = pl.ds(pl.multiple_of(side * HALF, 128), HALF)
            step = grad_ref[d].astype(f32) * scale
            weight = weight_ref[rows, lanes].astype(f32) - step_size * step
            update[rows, lanes] = step
            moved[rows, lanes] = weight.astype(bf16)
            after[rows, lanes] = ema_decay * ema_ref[rows, lanes] + (1.0 - ema_decay) * weight
        for k, (source, out) in enumerate(((update, update_out), (moved, moved_out), (after, next_out))):
            copies.append(pltpu.make_async_copy(source.at[rows, :], out.at[rows, :], sems.at[k, d]))
            copies[-1].start()
    for copy in copies:
        copy.wait()


def take_step(place, square_sum, mine, theirs, policy_weight, ema_weight):
    return pl.pallas_call(
        step_kernel,
        in_specs=[scalars()] + [whole()] * 5,
        out_specs=[in_place()] * 3,
        out_shape=[
            jax.ShapeDtypeStruct((SHARD, D_OUT), f32),
            jax.ShapeDtypeStruct((SHARD, D_OUT), bf16),
            jax.ShapeDtypeStruct((SHARD, D_OUT), f32),
        ],
        scratch_shapes=[
            VMEM((SHARD, D_OUT), f32),
            VMEM((SHARD, D_OUT), bf16),
            VMEM((SHARD, D_OUT), f32),
            pltpu.SemaphoreType.DMA((3, 4)),
        ],
        compiler_params=pltpu.CompilerParams(vmem_limit_bytes=24 * 1024 * 1024),
    )(place, square_sum, mine, theirs, policy_weight, ema_weight)


def local(
    q_policy,
    kv_policy,
    q_reference,
    kv_reference,
    target,
    send_slot,
    lengths,
    rewards,
    group_ids,
    policy_weight,
    ema_weight,
):
    place = jnp.stack([lax.axis_index(name) for name in EVERY]).astype(jnp.int32)
    c = place[2]
    send = lax.ppermute

    X = ("xl", "xh")

    def half(weight):
        return lax.dynamic_slice_in_dim(weight, c * HALF, HALF, 1).astype(bf16)

    p0, e0 = half(policy_weight), half(ema_weight)
    smp, spp, o0p = send(p0, "z", ring(1)), send(p0, "z", ring(-1)), send(p0, X, ACROSS)
    sme, spe, o0e = send(e0, "z", ring(1)), send(e0, "z", ring(-1)), send(e0, X, ACROSS)
    s2p, s2e = send(smp, "z", ring(1)), send(spe, "z", ring(-1))
    omp, ome = send(smp, X, ACROSS), send(sme, X, ACROSS)
    opp, ope = send(o0p, "z", ring(-1)), send(o0e, "z", ring(-1))
    o2p, o2e = send(s2p, X, ACROSS), send(ome, "z", ring(1))

    exchange = functools.partial(lax.all_to_all, axis_name=DP, split_axis=0, concat_axis=0, tiled=True)
    rows_policy = exchange(
        pack(
            pack_policy_kernel,
            FACTS_AT + 128,
            (send_slot, q_policy, kv_policy, target),
            small=(rewards, group_ids, lengths),
        )
    )
    rows_reference = exchange(
        pack(
            pack_rows_kernel,
            Q_WIDTH + 1024,
            (send_slot, q_reference, kv_reference),
            after=(rows_policy, smp, spp, o0p, sme, spe, o0e),
        )
    )
    out_policy = attend(rows_policy, lengths, ())
    other_policy = send(out_policy, "c", FLIP)
    out_reference = attend(rows_reference, lengths, (s2p, s2e, omp, ome, opp))
    other_reference = send(out_reference, "c", FLIP)

    facts = pl.pallas_call(
        facts_kernel,
        grid=(1,),
        in_specs=[pl.BlockSpec((ROWS, 128), lambda i: (0, FACTS_AT // 128))],
        out_specs=pl.BlockSpec((SPAN, 128), lambda i: (0, 0)),
        out_shape=jax.ShapeDtypeStruct((SPAN, 128), f32),
        compiler_params=SMALL,
    )(rows_policy)
    facts = jnp.concatenate([facts, send(facts, "xh", FLIP)], axis=0)
    facts = jnp.concatenate([facts] + [send(facts, "z", ring(d)) for d in (1, 2, 3)], axis=0)
    advantages = pl.pallas_call(
        advantage_kernel,
        in_specs=[scalars(), whole()],
        out_specs=whole(),
        out_shape=jax.ShapeDtypeStruct((8, 128), f32),
        compiler_params=SMALL,
    )(place, facts)

    outs = (out_policy, other_policy, out_reference, other_reference)
    parts = project_most(place, outs, (p0, spp, o0p, smp, s2p, omp, e0, spe, o0e, sme, s2e, ome))
    y_policy, stats = project_last(place, parts, (opp, o2p, ope, o2e), rows_policy)
    more = send(stats, "c", FLIP)
    first, second = gradient(
        place, out_policy, other_policy, y_policy, stats, more, rows_policy, advantages
    )

    first = [first[0]] + [send(first[d], "z", ring(d)) for d in (1, 2, 3)]
    second = [second[0]] + [send(second[d], "y", ring(d)) for d in (1, 2, 3)]
    first = sum_blocks(place, [piece.reshape(2, 4, 80, PIECE) for piece in first], 1, 0)
    second = sum_blocks(place, [piece.reshape(4, 2, 80, PIECE) for piece in second], 0, 3)
    first = [first[0]] + [send(first[d], "y", ring(d)) for d in (1, 2, 3)]
    second = [second[0]] + [send(second[d], "z", ring(d)) for d in (1, 2, 3)]
    kept, given = last_sum(place, first, second)

    def add(one, two):
        return (one.astype(f32) + two.astype(f32)).astype(bf16)

    block = add(kept, send(given, X, ACROSS))
    block = add(block, send(block, "xl", FLIP))

    mine = jnp.stack([block] + [send(block, "y", ring(-d)) for d in (1, 2, 3)])
    theirs = send(mine, "c", FLIP)
    square = jnp.sum(jnp.square(mine.astype(f32)), axis=(1, 2)) + jnp.sum(
        jnp.square(theirs.astype(f32)), axis=(1, 2)
    )
    square = (square[0] + square[2]) + (square[1] + square[3])
    square = jnp.broadcast_to(square, (8, 128))
    square = square + send(square, X, ACROSS)
    square = (square + send(square, "z", ring(2))) + (send(square, "z", ring(1)) + send(square, "z", ring(3)))
    return tuple(take_step(place, square, mine, theirs, policy_weight, ema_weight))


def solution(mesh):
    names = Mesh(mesh.devices.reshape(4, 2, 2, 4, 2), EVERY)
    rows, whole_rows = P(EVERY, None), P(EVERY)
    in_specs = (rows,) * 7 + (whole_rows,) * 2 + (P(FSDP, None),) * 2
    out_specs = (P(FSDP, None),) * 3
    return jax.shard_map(local, mesh=names, in_specs=in_specs, out_specs=out_specs, check_vma=False)
```

```python
import functools
import math

import jax
import jax.numpy as jnp
from jax import lax
from jax.experimental import pallas as pl
from jax.experimental.pallas import tpu as pltpu
from jax.sharding import Mesh
from jax.sharding import PartitionSpec as P

HEADS = 20
KV_HEADS = 4
HEAD_DIM = 128
D_OUT = 2560
GROUP = 8
Q_WIDTH = 2560
ROWS = 256
SPAN = 16
SHARD = 320
HALF = 1280
CHUNK = 256
WIDE = 640
PIECE = 640
LATE = 384
TARGET_AT = 2560
FACTS_AT = 3584

kl_weight = 0.1
step_size = 0.02
ema_decay = 0.95
std_floor = 0.6
norm_epsilon = 1e-06

bf16 = jnp.bfloat16
f32 = jnp.float32
VMEM = pltpu.VMEM
SMEM = pltpu.SMEM
BIG = pltpu.CompilerParams(vmem_limit_bytes=56 * 1024 * 1024)
SMALL = pltpu.CompilerParams(vmem_limit_bytes=24 * 1024 * 1024)

BRIEF = pl.CostEstimate(flops=1, bytes_accessed=1, transcendentals=0)

DP = ("y", "xl", "c")
FSDP = ("z", "xh")
EVERY = DP + FSDP


def ring(step):
    return [(i, (i + step) % 4) for i in range(4)]


FLIP = [(0, 1), (1, 0)]
ACROSS = [(2, 1), (1, 2), (0, 3), (3, 0)]


def whole(shape=None):
    return pl.BlockSpec(memory_space=VMEM)


def scalars():
    return pl.BlockSpec(memory_space=SMEM)


def in_place():
    return pl.BlockSpec(memory_space=pl.ANY)


def dot(a, b):
    return jnp.dot(a, b, preferred_element_type=f32)


def one_hot_rows(slots_ref):
    return (lax.broadcasted_iota(jnp.int32, (ROWS, ROWS), 0) == slots_ref[...]).astype(bf16)


def pack_rows_kernel(kv_at, slots_ref, q_ref, kv_ref, *rest):
    out_ref = rest[-1]
    pick = one_hot_rows(slots_ref)
    out_ref[:, :Q_WIDTH] = dot(pick, q_ref[...]).astype(bf16)
    out_ref[:, kv_at : kv_at + 1024] = dot(pick, kv_ref[...]).astype(bf16)


def pack_policy_kernel(rewards_ref, ids_ref, lengths_ref, slots_ref, q_ref, kv_ref, *rest):
    out_ref = rest[-1]
    pack_rows_kernel(Q_WIDTH, slots_ref, q_ref, kv_ref, out_ref)
    lane = lax.broadcasted_iota(jnp.int32, (8, 128), 1)
    facts = jnp.zeros((8, 128), f32)
    given = (rewards_ref[0], rewards_ref[1], ids_ref[0], ids_ref[1], lengths_ref[0, 0], lengths_ref[0, 1])
    for k, fact in enumerate(given):
        facts = jnp.where(lane % 8 == k, fact.astype(f32), facts)
    high = facts.astype(bf16).astype(f32)
    middle = (facts - high).astype(bf16).astype(f32)
    low = facts - high - middle
    coded = jnp.where(lane < 8, high, jnp.where(lane < 16, middle, low))
    out_ref[:, FACTS_AT:] = jnp.broadcast_to(coded[0:1], (ROWS, 128)).astype(bf16)


def pack_reference_kernel(slots_ref, q_ref, kv_ref, target_ref, *rest):
    out_ref = rest[-1]
    pack_rows_kernel(TARGET_AT + D_OUT, slots_ref, q_ref, kv_ref, out_ref)
    rows = dot(one_hot_rows(slots_ref), target_ref[...]).astype(bf16)
    left, right = slice(TARGET_AT, TARGET_AT + HALF), slice(TARGET_AT + HALF, TARGET_AT + D_OUT)
    for pair in range(ROWS // (2 * SPAN)):
        top = pair * 2 * SPAN
        one, two = slice(top, top + SPAN), slice(top + SPAN, top + 2 * SPAN)
        out_ref[one, left] = rows[one, :HALF]
        out_ref[one, right] = rows[two, :HALF]
        out_ref[two, left] = rows[one, HALF:]
        out_ref[two, right] = rows[two, HALF:]


def pack(kernel, width, operands, after=(), small=()):
    return pl.pallas_call(
        kernel,
        in_specs=[scalars()] * len(small) + [whole()] * len(operands) + [in_place()] * len(after),
        out_specs=whole(),
        out_shape=jax.ShapeDtypeStruct((ROWS, width), bf16),
        compiler_params=BIG,
        cost_estimate=BRIEF,
    )(*small, *operands, *after)


def gate_kernel(rows_ref, *rest):
    pass


def hold(rows, after):
    return pl.pallas_call(
        gate_kernel,
        in_specs=[in_place()] * (1 + len(after)),
        out_specs=in_place(),
        out_shape=jax.ShapeDtypeStruct(rows.shape, rows.dtype),
        input_output_aliases={0: 0},
    )(rows, *after)


def attention_kernel(lengths_ref, q_ref, k_ref, v_ref, *rest):
    out_ref = rest[-1]
    row = lax.broadcasted_iota(jnp.int32, (ROWS, ROWS), 0)
    column = lax.broadcasted_iota(jnp.int32, (ROWS, ROWS), 1)
    bound = lengths_ref[0, 0]
    allowed = (column <= row) & ((column >= bound) | (row < bound))
    keys, values = k_ref[...], v_ref[...]
    for head in range(HEADS // KV_HEADS):
        lanes = slice(head * HEAD_DIM, (head + 1) * HEAD_DIM)
        scores = lax.dot_general(
            q_ref[:, lanes], keys, (((1,), (1,)), ((), ())), preferred_element_type=f32
        ) * (1.0 / math.sqrt(HEAD_DIM))
        scores = jnp.where(allowed, scores, -1e30)
        weights = jnp.exp(scores - jnp.max(scores, axis=1, keepdims=True))
        shares = (weights / jnp.sum(weights, axis=1, keepdims=True)).astype(bf16)
        out_ref[:, lanes] = dot(shares, values).astype(bf16)


def attend(rows, lengths, kv_at, after=()):
    q_at, k_at, v_at = 0, kv_at, kv_at + 512
    width = Q_WIDTH // KV_HEADS
    return pl.pallas_call(
        attention_kernel,
        grid=(KV_HEADS,),
        in_specs=[
            scalars(),
            pl.BlockSpec((ROWS, width), lambda g: (0, q_at // width + g)),
            pl.BlockSpec((ROWS, HEAD_DIM), lambda g: (0, k_at // HEAD_DIM + g)),
            pl.BlockSpec((ROWS, HEAD_DIM), lambda g: (0, v_at // HEAD_DIM + g)),
        ]
        + [in_place()] * len(after),
        out_specs=pl.BlockSpec((ROWS, width), lambda g: (0, g)),
        out_shape=jax.ShapeDtypeStruct((ROWS, Q_WIDTH), bf16),
        compiler_params=BIG,
        cost_estimate=BRIEF,
    )(lengths, rows, rows, rows, *after)


def facts_kernel(coded_ref, out_ref):
    for block in range(ROWS // SPAN):
        coded = coded_ref[block * SPAN : (block + 1) * SPAN, :].astype(f32)[:8]
        facts = coded + pltpu.roll(coded, 128 - 8, 1) + pltpu.roll(coded, 128 - 16, 1)
        out_ref[block : block + 1, :] = facts[0:1]


def advantage_kernel(place_ref, facts_ref, out_ref):
    facts = facts_ref[...]
    row = lax.broadcasted_iota(jnp.int32, facts.shape, 0)
    lane = lax.broadcasted_iota(jnp.int32, facts.shape, 1)
    ids = pltpu.roll(facts, 128 - 2, 1)
    chip = (place_ref[3] * 2 + place_ref[4]) * SPAN + place_ref[0] * 4 + place_ref[1] * 2
    own, other = chip + place_ref[2], chip + 1 - place_ref[2]

    def fact(device, at):
        return jnp.sum(jnp.where((row == device) & (lane == at), facts, 0.0))

    for j in range(4):
        device, mine = (own, other)[j // 2], j % 2
        reward, group = fact(device, mine), fact(device, 2 + mine)
        held = jnp.where((lane < 2) & (ids == group), facts, 0.0)
        center = jnp.sum(held, keepdims=True) / GROUP
        second = jnp.sum(held * held, keepdims=True) / GROUP
        spread = jnp.maximum(jnp.sqrt(jnp.maximum(second - center * center, 0.0)), std_floor)
        out_ref[j : j + 1, :] = jnp.broadcast_to((reward - center) / spread, (1, 128))
        out_ref[4 + j : 5 + j, :] = jnp.full((1, 128), fact(device, 4 + mine), f32)


def project_most_kernel(
    place_ref, own_p, other_p, own_r, other_r, w0, sm, sp, s2, o0, om, op,
    y_p, y_r, late_p, late_r, rows_p, rows_r, weight_p, weight_r, sems,
):
    z, xh = place_ref[3], place_ref[4]
    here, there = xh, 1 - xh

    def place_of(dz, side):
        return pl.multiple_of((lax.rem(z + 4 + dz, 4) * 2 + side) * SHARD, 64)

    blocks = (
        (w0, 0, here), (sm, -1, here), (sp, 1, here), (s2, 2, here),
        (o0, 0, there), (om, -1, there), (op, 1, there),
    )
    copies = []
    for k, (own, other, rows, weight) in enumerate(
        ((own_p, other_p, rows_p, weight_p), (own_r, other_r, rows_r, weight_r))
    ):
        group = [
            pltpu.make_async_copy(own, rows.at[pl.ds(0, ROWS), :], sems.at[k]),
            pltpu.make_async_copy(other, rows.at[pl.ds(ROWS, ROWS), :], sems.at[k]),
        ]
        for block, dz, side in blocks:
            group.append(
                pltpu.make_async_copy(
                    block.at[pl.ds(k * SHARD, SHARD), :],
                    weight.at[pl.ds(place_of(dz, side), SHARD), :],
                    sems.at[k],
                )
            )
        for copy in group:
            copy.start()
        copies.append(group)
    for weight in (weight_p, weight_r):
        weight[pl.ds(place_of(2, there), SHARD), :] = jnp.zeros((SHARD, HALF), bf16)

    def run(rows, weight, out, late):
        def step(j, carry):
            at = pl.multiple_of(j * CHUNK, CHUNK)
            out[:, pl.ds(at, CHUNK)] = dot(rows[...], weight[:, pl.ds(at, CHUNK)])
            return carry

        lax.fori_loop(0, HALF // CHUNK, step, 0)
        part = rows[:, pl.ds(pl.multiple_of(lax.rem(z + 2, 4) * PIECE, 128), PIECE)].astype(f32)
        part = jnp.where(there == 0, part, pltpu.roll(part, PIECE - SHARD, 1))
        late[...] = part[:, :LATE].astype(bf16)

    for copy in copies[0]:
        copy.wait()
    run(rows_p, weight_p, y_p, late_p)
    for copy in copies[1]:
        copy.wait()
    run(rows_r, weight_r, y_r, late_r)


def project_most(place, outs, weights):
    return pl.pallas_call(
        project_most_kernel,
        in_specs=[scalars()] + [in_place()] * (len(outs) + len(weights)),
        out_specs=[whole()] * 4,
        out_shape=[jax.ShapeDtypeStruct((2 * ROWS, HALF), f32)] * 2
        + [jax.ShapeDtypeStruct((2 * ROWS, LATE), bf16)] * 2,
        scratch_shapes=[
            VMEM((2 * ROWS, Q_WIDTH), bf16),
            VMEM((2 * ROWS, Q_WIDTH), bf16),
            VMEM((Q_WIDTH, HALF), bf16),
            VMEM((Q_WIDTH, HALF), bf16),
            pltpu.SemaphoreType.DMA((2,)),
        ],
        compiler_params=BIG,
        cost_estimate=BRIEF,
    )(place, *outs, *weights)


def lanes_of(value):
    total = value[:, :128]
    for k in range(1, value.shape[1] // 128):
        total = total + value[:, k * 128 : (k + 1) * 128]
    return total


def project_last_kernel(
    place_ref, rows_p, rows_r, o2p, o2e, y_p, y_r, mine_ref, theirs_ref,
    y_ref, stats_ref, late_p, late_r, sums,
):
    j = pl.program_id(0)

    @pl.when(j == 0)
    def _():
        sums[...] = jnp.zeros_like(sums)
        for late in (late_p, late_r):
            late[SHARD:, :] = jnp.zeros((LATE - SHARD, WIDE), bf16)

    late_p[:SHARD, :] = o2p[...]
    late_r[:SHARD, :] = o2e[...]

    target = jnp.concatenate([mine_ref[...], theirs_ref[...]], axis=0).astype(f32)
    y = y_p[...] + dot(rows_p[...], late_p[...])
    y_ref[...] = y
    sums[0] += lanes_of(y * y)
    sums[1] += lanes_of(y * target)
    y = y_r[...] + dot(rows_r[...], late_r[...])
    sums[2] += lanes_of(y * y)
    sums[3] += lanes_of(y * target)

    @pl.when(j == HALF // WIDE - 1)
    def _():
        lane = lax.broadcasted_iota(jnp.int32, (2 * ROWS, 128), 1)
        stats = jnp.zeros((2 * ROWS, 128), f32)
        for k in range(4):
            stats = jnp.where(lane == k, jnp.sum(sums[k], axis=1, keepdims=True), stats)
        stats_ref[...] = stats


def project_last(place, parts, weights, target):
    steps = HALF // WIDE
    chunk = lambda rows: pl.BlockSpec((rows, WIDE), lambda j, place: (0, j))
    fixed = lambda width: pl.BlockSpec((2 * ROWS, width), lambda j, place: (0, 0))
    y_p, y_r, rows_p, rows_r = parts
    return pl.pallas_call(
        project_last_kernel,
        grid_spec=pltpu.PrefetchScalarGridSpec(
            num_scalar_prefetch=1,
            grid=(steps,),
            in_specs=[fixed(LATE)] * 2
            + [chunk(SHARD)] * 2
            + [chunk(2 * ROWS)] * 2
            + [
                pl.BlockSpec((ROWS, WIDE), lambda j, place: (0, TARGET_AT // WIDE + place[2] * steps + j)),
                pl.BlockSpec((ROWS, WIDE), lambda j, place: (0, TARGET_AT // WIDE + (1 - place[2]) * steps + j)),
            ],
            out_specs=[chunk(2 * ROWS), fixed(128)],
            scratch_shapes=[
                VMEM((LATE, WIDE), bf16),
                VMEM((LATE, WIDE), bf16),
                VMEM((4, 2 * ROWS, 128), f32),
            ],
        ),
        out_shape=[
            jax.ShapeDtypeStruct((2 * ROWS, HALF), f32),
            jax.ShapeDtypeStruct((2 * ROWS, 128), f32),
        ],
        compiler_params=BIG,
        cost_estimate=pl.CostEstimate(
            flops=2 * ROWS * Q_WIDTH * HALF, bytes_accessed=10 << 20, transcendentals=0
        ),
    )(place, rows_p, rows_r, *weights, y_p, y_r, target, target)


def gradient_kernel(
    place_ref, own_ref, other_ref, y_ref, stats_ref, more_ref, mine_ref, theirs_ref, facts_ref,
    a0, a1, a2, a3, grad, rows,
):
    z = place_ref[3]
    rows[:ROWS, :] = own_ref[...]
    rows[ROWS:, :] = other_ref[...]
    row = lax.broadcasted_iota(jnp.int32, (ROWS, 1), 0)
    for side in range(2):
        here = slice(side * ROWS, (side + 1) * ROWS)
        there = slice((1 - side) * ROWS, (2 - side) * ROWS)
        stats = stats_ref[here, :] + more_ref[there, :]
        policy_squares, policy_products = stats[:, 0:1], stats[:, 1:2]
        reference_squares, reference_products = stats[:, 2:3], stats[:, 3:4]
        one, two = 2 * side, 2 * side + 1
        early = row.astype(f32) < facts_ref[4 + one : 5 + one, 0:1]
        length = jnp.where(early, facts_ref[4 + one : 5 + one, 0:1], facts_ref[4 + two : 5 + two, 0:1])
        advantage = jnp.where(early, facts_ref[one : one + 1, 0:1], facts_ref[two : two + 1, 0:1])
        policy_norm = jnp.sqrt(policy_squares / D_OUT + norm_epsilon)
        reference_norm = jnp.sqrt(reference_squares / D_OUT + norm_epsilon)
        policy_self = policy_squares / (policy_norm * policy_norm)
        policy_cross = policy_products / policy_norm
        reference_self = reference_squares / (reference_norm * reference_norm)
        reference_cross = reference_products / reference_norm
        gain = ((policy_self - reference_self) - 2.0 * (policy_cross - reference_cross)) * (
            1.0 / (4.0 * math.sqrt(D_OUT))
        )
        weight = (advantage - kl_weight * (1.0 - jnp.exp(gain))) / length
        along = (policy_self - policy_cross) / D_OUT
        scale = weight / policy_norm
        slope = scale * (1.0 - along) / policy_norm
        target = (mine_ref if side == 0 else theirs_ref)[...].astype(f32)
        grad[here, :] = (y_ref[here, :] * slope - target * scale).astype(bf16)

    for d, out in enumerate((a0, a1, a2, a3)):
        first = pl.multiple_of(lax.rem(z + d, 4) * PIECE, 128)
        out[...] = outer(rows[:, pl.ds(first, PIECE)], grad[:, :PIECE])


def outer(rows, grad):
    return lax.dot_general(rows, grad, (((0,), (0,)), ((), ())), preferred_element_type=f32).astype(bf16)


def second_half_kernel(place_ref, own_ref, other_ref, grad_ref, b0, b1, b2, b3, rows, terms):
    rows[:ROWS, :] = own_ref[...]
    rows[ROWS:, :] = other_ref[...]
    for k in range(4):
        terms[...] = outer(rows[:, k * PIECE : (k + 1) * PIECE], grad_ref[:, PIECE:]).reshape(2, 4, 80, PIECE)
        for d, out in enumerate((b0, b1, b2, b3)):
            out[2 * k : 2 * k + 2] = terms[:, lax.rem(place_ref[0] + d, 4)]


def gradient(place, own, other, y, stats, more, target, facts):
    cost = pl.CostEstimate(flops=2 * ROWS * Q_WIDTH * HALF, bytes_accessed=8 << 20, transcendentals=0)
    *first, grad = pl.pallas_call(
        gradient_kernel,
        grid_spec=pltpu.PrefetchScalarGridSpec(
            num_scalar_prefetch=1,
            grid=(1,),
            in_specs=[whole()] * 5
            + [
                pl.BlockSpec((ROWS, HALF), lambda i, place: (0, TARGET_AT // HALF + place[2])),
                pl.BlockSpec((ROWS, HALF), lambda i, place: (0, TARGET_AT // HALF + 1 - place[2])),
                whole(),
            ],
            out_specs=[whole()] * 5,
            scratch_shapes=[VMEM((2 * ROWS, Q_WIDTH), bf16)],
        ),
        out_shape=[jax.ShapeDtypeStruct((PIECE, PIECE), bf16)] * 4
        + [jax.ShapeDtypeStruct((2 * ROWS, HALF), bf16)],
        compiler_params=SMALL,
        cost_estimate=cost,
    )(place, own, other, y, stats, more, target, target, facts)
    second = pl.pallas_call(
        second_half_kernel,
        in_specs=[scalars()] + [whole()] * 3,
        out_specs=[whole()] * 4,
        out_shape=[jax.ShapeDtypeStruct((8, 80, PIECE), bf16)] * 4,
        scratch_shapes=[VMEM((2 * ROWS, Q_WIDTH), bf16), VMEM((2, 4, 80, PIECE), bf16)],
        compiler_params=SMALL,
        cost_estimate=cost,
    )(place, own, other, grad)
    return first, second


def total_of(refs, index):
    total = refs[0][index].astype(f32)
    for ref in refs[1:]:
        total = total + ref[index].astype(f32)
    return total


def sum_kernel(axis, place_at, place_ref, *refs):
    parts, outs = refs[:4], refs[4:]
    own = place_ref[place_at]
    for d, out in enumerate(outs):
        at = lax.rem(own + d, 4)
        index = (slice(None), at) if axis == 1 else (at,)
        out[...] = total_of(parts, index).astype(bf16)


def sum_blocks(place, parts, axis, place_at):
    shape = (2, 80, PIECE)
    return pl.pallas_call(
        functools.partial(sum_kernel, axis, place_at),
        in_specs=[scalars()] + [whole()] * 4,
        out_specs=[whole()] * 4,
        out_shape=[jax.ShapeDtypeStruct(shape, bf16)] * 4,
        compiler_params=SMALL,
        cost_estimate=pl.CostEstimate(flops=4 << 20, bytes_accessed=5 << 20, transcendentals=0),
    )(place, *parts)


def last_sum_kernel(place_ref, *refs):
    first, second, keep, send = refs[:4], refs[4:8], refs[8], refs[9]
    xh = place_ref[4]
    for out, at in ((keep, xh), (send, 1 - xh)):
        out[:, :PIECE] = total_of(first, (at,)).astype(bf16)
        out[:, PIECE:] = total_of(second, (at,)).astype(bf16)


def last_sum(place, first, second):
    return pl.pallas_call(
        last_sum_kernel,
        in_specs=[scalars()] + [whole()] * 8,
        out_specs=[whole()] * 2,
        out_shape=[jax.ShapeDtypeStruct((80, HALF), bf16)] * 2,
        compiler_params=SMALL,
    )(place, *first, *second)


def step_kernel(
    place_ref, square_ref, mine_ref, theirs_ref, weight_ref, ema_ref,
    update_out, moved_out, next_out, update, moved, after, sems,
):
    scale = lax.rsqrt(square_ref[0:1, 0:1] / (Q_WIDTH * D_OUT) + norm_epsilon)
    y_at, c = place_ref[0], place_ref[2]
    copies = []
    for d in range(4):
        rows = pl.ds(pl.multiple_of(lax.rem(y_at + d, 4) * 80, 16), 80)
        for side, grad_ref in ((c, mine_ref), (1 - c, theirs_ref)):
            lanes = pl.ds(pl.multiple_of(side * HALF, 128), HALF)
            step = grad_ref[d].astype(f32) * scale
            weight = weight_ref[rows, lanes].astype(f32) - step_size * step
            update[rows, lanes] = step
            moved[rows, lanes] = weight.astype(bf16)
            after[rows, lanes] = ema_decay * ema_ref[rows, lanes] + (1.0 - ema_decay) * weight
        for k, (source, out) in enumerate(((update, update_out), (moved, moved_out), (after, next_out))):
            copies.append(pltpu.make_async_copy(source.at[rows, :], out.at[rows, :], sems.at[k, d]))
            copies[-1].start()
    for copy in copies:
        copy.wait()


def square_kernel(mine_ref, theirs_ref, out_ref):
    def block(d):
        mine, theirs = mine_ref[d].astype(f32), theirs_ref[d].astype(f32)
        return jnp.sum(mine * mine, keepdims=True) + jnp.sum(theirs * theirs, keepdims=True)

    total = (block(0) + block(2)) + (block(1) + block(3))
    out_ref[...] = jnp.broadcast_to(total, (8, 128))


def take_step(place, square_sum, mine, theirs, policy_weight, ema_weight):
    return pl.pallas_call(
        step_kernel,
        in_specs=[scalars()] + [whole()] * 5,
        out_specs=[in_place()] * 3,
        out_shape=[
            jax.ShapeDtypeStruct((SHARD, D_OUT), f32),
            jax.ShapeDtypeStruct((SHARD, D_OUT), bf16),
            jax.ShapeDtypeStruct((SHARD, D_OUT), f32),
        ],
        scratch_shapes=[
            VMEM((SHARD, D_OUT), f32),
            VMEM((SHARD, D_OUT), bf16),
            VMEM((SHARD, D_OUT), f32),
            pltpu.SemaphoreType.DMA((3, 4)),
        ],
        compiler_params=pltpu.CompilerParams(vmem_limit_bytes=24 * 1024 * 1024),
    )(place, square_sum, mine, theirs, policy_weight, ema_weight)


def local(
    q_policy,
    kv_policy,
    q_reference,
    kv_reference,
    target,
    send_slot,
    lengths,
    rewards,
    group_ids,
    policy_weight,
    ema_weight,
):
    place = jnp.stack([lax.axis_index(name) for name in EVERY]).astype(jnp.int32)
    c = place[2]
    send = lax.ppermute

    X = ("xl", "xh")

    def half(weight):
        return lax.dynamic_slice_in_dim(weight, c * HALF, HALF, 1).astype(bf16)

    w0 = jnp.concatenate([half(policy_weight), half(ema_weight)], axis=0)
    sm, sp, o0 = send(w0, "z", ring(1)), send(w0, "z", ring(-1)), send(w0, X, ACROSS)
    s2, op, om = send(sm, "z", ring(1)), send(o0, "z", ring(-1)), send(sm, X, ACROSS)
    o2p, o2e = send(s2[:SHARD], X, ACROSS), send(om[SHARD:], "z", ring(1))

    exchange = functools.partial(lax.all_to_all, axis_name=DP, split_axis=0, concat_axis=0, tiled=True)
    rows_policy = exchange(
        pack(
            pack_policy_kernel,
            FACTS_AT + 128,
            (send_slot, q_policy, kv_policy),
            small=(rewards, group_ids, lengths),
            after=(w0,),
        )
    )
    packed = pack(
        pack_reference_kernel, Q_WIDTH + D_OUT + 1024, (send_slot, q_reference, kv_reference, target)
    )
    rows_reference = exchange(hold(packed, (rows_policy, sm, sp, o0)))
    out_policy = attend(rows_policy, lengths, Q_WIDTH)
    other_policy = send(out_policy, "c", FLIP)
    facts = pl.pallas_call(
        facts_kernel,
        grid=(1,),
        in_specs=[pl.BlockSpec((ROWS, 128), lambda i: (0, FACTS_AT // 128))],
        out_specs=pl.BlockSpec((SPAN, 128), lambda i: (0, 0)),
        out_shape=jax.ShapeDtypeStruct((SPAN, 128), f32),
        compiler_params=SMALL,
    )(rows_policy)
    facts = jnp.broadcast_to(facts[None], (8, SPAN, 128)).reshape(8 * SPAN, 128)
    facts = lax.all_to_all(facts, FSDP, split_axis=0, concat_axis=0, tiled=True)
    advantages = pl.pallas_call(
        advantage_kernel,
        in_specs=[scalars(), whole()],
        out_specs=whole(),
        out_shape=jax.ShapeDtypeStruct((8, 128), f32),
        compiler_params=SMALL,
    )(place, facts)

    out_reference = attend(rows_reference, lengths, TARGET_AT + D_OUT, (advantages,))
    other_reference = send(out_reference, "c", FLIP)

    outs = (out_policy, other_policy, out_reference, other_reference)
    parts = project_most(place, outs, (w0, sm, sp, s2, o0, om, op))
    y_policy, stats = project_last(place, parts, (o2p, o2e), rows_reference)
    more = send(stats, "c", FLIP)
    first, second = gradient(
        place, out_policy, other_policy, y_policy, stats, more, rows_reference, advantages
    )

    first = [first[0]] + [send(first[d], "z", ring(d)) for d in (1, 2, 3)]
    near = send(second[1], "y", ring(1))
    far = send(hold(second[2], (near,)), "y", ring(2))
    second = [second[0], near, far, send(second[3], "y", ring(3))]
    first = sum_blocks(place, [piece.reshape(2, 4, 80, PIECE) for piece in first], 1, 0)
    second = sum_blocks(place, [piece.reshape(4, 2, 80, PIECE) for piece in second], 0, 3)
    first = [first[0]] + [send(first[d], "y", ring(d)) for d in (1, 2, 3)]
    second = [second[0]] + [send(second[d], "z", ring(d)) for d in (1, 2, 3)]
    kept, given = last_sum(place, first, second)

    def add(one, two):
        return (one.astype(f32) + two.astype(f32)).astype(bf16)

    block = add(kept, send(given, X, ACROSS))
    block = add(block, send(block, "xl", FLIP))

    mine = jnp.stack([block] + [send(block, "y", ring(-d)) for d in (1, 2, 3)])
    theirs = send(mine, "c", FLIP)
    square = pl.pallas_call(
        square_kernel,
        in_specs=[whole()] * 2,
        out_specs=whole(),
        out_shape=jax.ShapeDtypeStruct((8, 128), f32),
        compiler_params=SMALL,
    )(mine, theirs)
    square = square + send(square, X, ACROSS)
    square = (square + send(square, "z", ring(2))) + (send(square, "z", ring(1)) + send(square, "z", ring(3)))
    return tuple(take_step(place, square, mine, theirs, policy_weight, ema_weight))


def solution(mesh):
    names = Mesh(mesh.devices.reshape(4, 2, 2, 4, 2), EVERY)
    rows, whole_rows = P(EVERY, None), P(EVERY)
    in_specs = (rows,) * 7 + (whole_rows,) * 2 + (P(FSDP, None),) * 2
    out_specs = (P(FSDP, None),) * 3
    return jax.shard_map(local, mesh=names, in_specs=in_specs, out_specs=out_specs, check_vma=False)
```

```python
import functools
import math

import jax
import jax.numpy as jnp
from jax import lax
from jax.experimental import pallas as pl
from jax.experimental.pallas import tpu as pltpu
from jax.sharding import Mesh
from jax.sharding import PartitionSpec as P

HEADS = 20
KV_HEADS = 4
HEAD_DIM = 128
D_OUT = 2560
GROUP = 8
Q_WIDTH = 2560
ROWS = 256
SPAN = 16
SHARD = 320
HALF = 1280
CHUNK = 256
WIDE = 640
PIECE = 640
LATE = 384
TARGET_AT = 2560
FACTS_AT = 6144

kl_weight = 0.1
step_size = 0.02
ema_decay = 0.95
std_floor = 0.6
norm_epsilon = 1e-06

bf16 = jnp.bfloat16
f32 = jnp.float32
VMEM = pltpu.VMEM
SMEM = pltpu.SMEM
BIG = pltpu.CompilerParams(vmem_limit_bytes=56 * 1024 * 1024)
HUGE = pltpu.CompilerParams(vmem_limit_bytes=63 * 1024 * 1024)
SMALL = pltpu.CompilerParams(vmem_limit_bytes=24 * 1024 * 1024)

BRIEF = pl.CostEstimate(flops=1, bytes_accessed=1, transcendentals=0)

DP = ("y", "xl", "c")
FSDP = ("z", "xh")
EVERY = DP + FSDP


def ring(step):
    return [(i, (i + step) % 4) for i in range(4)]


FLIP = [(0, 1), (1, 0)]
ACROSS = [(2, 1), (1, 2), (0, 3), (3, 0)]


def whole(shape=None):
    return pl.BlockSpec(memory_space=VMEM)


def scalars():
    return pl.BlockSpec(memory_space=SMEM)


def in_place():
    return pl.BlockSpec(memory_space=pl.ANY)


def dot(a, b):
    return jnp.dot(a, b, preferred_element_type=f32)


def one_hot_rows(slots_ref):
    return (lax.broadcasted_iota(jnp.int32, (ROWS, ROWS), 0) == slots_ref[...]).astype(bf16)


def pack_rows_kernel(kv_at, slots_ref, q_ref, kv_ref, *rest):
    out_ref = rest[-1]
    pick = one_hot_rows(slots_ref)
    out_ref[:, :Q_WIDTH] = dot(pick, q_ref[...]).astype(bf16)
    out_ref[:, kv_at : kv_at + 1024] = dot(pick, kv_ref[...]).astype(bf16)


def pack_policy_kernel(rewards_ref, ids_ref, lengths_ref, slots_ref, q_ref, kv_ref, target_ref, *rest):
    out_ref = rest[-1]
    pack_rows_kernel(TARGET_AT + D_OUT, slots_ref, q_ref, kv_ref, out_ref)
    rows = dot(one_hot_rows(slots_ref), target_ref[...]).astype(bf16)
    left, right = slice(TARGET_AT, TARGET_AT + HALF), slice(TARGET_AT + HALF, TARGET_AT + D_OUT)
    for pair in range(ROWS // (2 * SPAN)):
        top = pair * 2 * SPAN
        one, two = slice(top, top + SPAN), slice(top + SPAN, top + 2 * SPAN)
        out_ref[one, left] = rows[one, :HALF]
        out_ref[one, right] = rows[two, :HALF]
        out_ref[two, left] = rows[one, HALF:]
        out_ref[two, right] = rows[two, HALF:]
    lane = lax.broadcasted_iota(jnp.int32, (8, 128), 1)
    facts = jnp.zeros((8, 128), f32)
    given = (rewards_ref[0], rewards_ref[1], ids_ref[0], ids_ref[1], lengths_ref[0, 0], lengths_ref[0, 1])
    for k, fact in enumerate(given):
        facts = jnp.where(lane % 8 == k, fact.astype(f32), facts)
    high = facts.astype(bf16).astype(f32)
    middle = (facts - high).astype(bf16).astype(f32)
    low = facts - high - middle
    coded = jnp.where(lane < 8, high, jnp.where(lane < 16, middle, low))
    out_ref[:, FACTS_AT:] = jnp.broadcast_to(coded[0:1], (ROWS, 128)).astype(bf16)


def pack(kernel, width, operands, after=(), small=()):
    return pl.pallas_call(
        kernel,
        in_specs=[scalars()] * len(small) + [whole()] * len(operands) + [in_place()] * len(after),
        out_specs=whole(),
        out_shape=jax.ShapeDtypeStruct((ROWS, width), bf16),
        compiler_params=BIG,
        cost_estimate=BRIEF,
    )(*small, *operands, *after)


def gate_kernel(rows_ref, *rest):
    pass


def hold(rows, after):
    return pl.pallas_call(
        gate_kernel,
        in_specs=[in_place()] * (1 + len(after)),
        out_specs=in_place(),
        out_shape=jax.ShapeDtypeStruct(rows.shape, rows.dtype),
        input_output_aliases={0: 0},
    )(rows, *after)


def halves_kernel(first_ref, second_ref, policy_ref, averaged_ref):
    policy_ref[...] = first_ref[...]
    averaged_ref[...] = second_ref[...]


def halves(first, second):
    part = lambda at: pl.BlockSpec((SHARD, HALF), lambda i: (at, 0))
    return pl.pallas_call(
        halves_kernel,
        grid=(1,),
        in_specs=[part(0), part(1)],
        out_specs=[part(0)] * 2,
        out_shape=[jax.ShapeDtypeStruct((SHARD, HALF), bf16)] * 2,
        compiler_params=BIG,
    )(first, second)


def attention_kernel(lengths_ref, q_ref, k_ref, v_ref, *rest):
    out_ref = rest[-1]
    row = lax.broadcasted_iota(jnp.int32, (ROWS, ROWS), 0)
    column = lax.broadcasted_iota(jnp.int32, (ROWS, ROWS), 1)
    bound = lengths_ref[0, 0]
    allowed = (column <= row) & ((column >= bound) | (row < bound))
    keys, values = k_ref[...], v_ref[...]
    for head in range(HEADS // KV_HEADS):
        lanes = slice(head * HEAD_DIM, (head + 1) * HEAD_DIM)
        scores = lax.dot_general(
            q_ref[:, lanes], keys, (((1,), (1,)), ((), ())), preferred_element_type=f32
        ) * (1.0 / math.sqrt(HEAD_DIM))
        scores = jnp.where(allowed, scores, -1e30)
        weights = jnp.exp(scores - jnp.max(scores, axis=1, keepdims=True))
        shares = (weights / jnp.sum(weights, axis=1, keepdims=True)).astype(bf16)
        out_ref[:, lanes] = dot(shares, values).astype(bf16)


def attend(rows, lengths, kv_at, after=()):
    q_at, k_at, v_at = 0, kv_at, kv_at + 512
    width = Q_WIDTH // KV_HEADS
    return pl.pallas_call(
        attention_kernel,
        grid=(KV_HEADS,),
        in_specs=[
            scalars(),
            pl.BlockSpec((ROWS, width), lambda g: (0, q_at // width + g)),
            pl.BlockSpec((ROWS, HEAD_DIM), lambda g: (0, k_at // HEAD_DIM + g)),
            pl.BlockSpec((ROWS, HEAD_DIM), lambda g: (0, v_at // HEAD_DIM + g)),
        ]
        + [in_place()] * len(after),
        out_specs=pl.BlockSpec((ROWS, width), lambda g: (0, g)),
        out_shape=jax.ShapeDtypeStruct((ROWS, Q_WIDTH), bf16),
        compiler_params=BIG,
        cost_estimate=BRIEF,
    )(lengths, rows, rows, rows, *after)


def facts_kernel(coded_ref, out_ref):
    for block in range(ROWS // SPAN):
        coded = coded_ref[block * SPAN : (block + 1) * SPAN, :].astype(f32)[:8]
        facts = coded + pltpu.roll(coded, 128 - 8, 1) + pltpu.roll(coded, 128 - 16, 1)
        out_ref[block : block + 1, :] = facts[0:1]


def advantage_kernel(place_ref, one, two, three, four, out_ref):
    facts = jnp.concatenate([one[...], two[...], three[...], four[...]], axis=0)
    row = lax.broadcasted_iota(jnp.int32, facts.shape, 0)
    lane = lax.broadcasted_iota(jnp.int32, facts.shape, 1)
    ids = pltpu.roll(facts, 128 - 2, 1)
    chip = place_ref[0] * 4 + place_ref[1] * 2
    own, other = chip + place_ref[2], chip + 1 - place_ref[2]

    def fact(device, at):
        return jnp.sum(jnp.where((row == device) & (lane == at), facts, 0.0))

    for j in range(4):
        device, mine = (own, other)[j // 2], j % 2
        reward, group = fact(device, mine), fact(device, 2 + mine)
        held = jnp.where((lane < 2) & (ids == group), facts, 0.0)
        center = jnp.sum(held, keepdims=True) / GROUP
        second = jnp.sum(held * held, keepdims=True) / GROUP
        spread = jnp.maximum(jnp.sqrt(jnp.maximum(second - center * center, 0.0)), std_floor)
        out_ref[j : j + 1, :] = jnp.broadcast_to((reward - center) / spread, (1, 128))
        out_ref[4 + j : 5 + j, :] = jnp.full((1, 128), fact(device, 4 + mine), f32)


def project_most_kernel(
    place_ref, own_p, other_p, own_r, other_r, w0, sm, sp, s2, o0, om, op, after,
    y_p, y_r, late_p, late_r, rows_p, rows_r, weight_p, weight_r, sems,
):
    z, xh = place_ref[3], place_ref[4]
    here, there = xh, 1 - xh

    def place_of(dz, side):
        return pl.multiple_of((lax.rem(z + 4 + dz, 4) * 2 + side) * SHARD, 64)

    blocks = (
        (w0, 0, here), (sm, -1, here), (sp, 1, here), (s2, 2, here),
        (o0, 0, there), (om, -1, there), (op, 1, there),
    )
    copies = []
    for k, (own, other, rows, weight) in enumerate(
        ((own_p, other_p, rows_p, weight_p), (own_r, other_r, rows_r, weight_r))
    ):
        group = [
            pltpu.make_async_copy(own, rows.at[pl.ds(0, ROWS), :], sems.at[k]),
            pltpu.make_async_copy(other, rows.at[pl.ds(ROWS, ROWS), :], sems.at[k]),
        ]
        for block, dz, side in blocks:
            group.append(
                pltpu.make_async_copy(
                    block.at[pl.ds(k * SHARD, SHARD), :],
                    weight.at[pl.ds(place_of(dz, side), SHARD), :],
                    sems.at[k],
                )
            )
        for copy in group:
            copy.start()
        copies.append(group)
    for weight in (weight_p, weight_r):
        weight[pl.ds(place_of(2, there), SHARD), :] = jnp.zeros((SHARD, HALF), bf16)

    def run(rows, weight, out, late):
        def step(j, carry):
            at = pl.multiple_of(j * CHUNK, CHUNK)
            out[:, pl.ds(at, CHUNK)] = dot(rows[...], weight[:, pl.ds(at, CHUNK)])
            return carry

        lax.fori_loop(0, HALF // CHUNK, step, 0)
        part = rows[:, pl.ds(pl.multiple_of(lax.rem(z + 2, 4) * PIECE, 128), PIECE)].astype(f32)
        part = jnp.where(there == 0, part, pltpu.roll(part, PIECE - SHARD, 1))
        late[...] = part[:, :LATE].astype(bf16)

    for copy in copies[0]:
        copy.wait()
    run(rows_p, weight_p, y_p, late_p)
    for copy in copies[1]:
        copy.wait()
    run(rows_r, weight_r, y_r, late_r)


def project_most(place, outs, weights):
    return pl.pallas_call(
        project_most_kernel,
        in_specs=[scalars()] + [in_place()] * (len(outs) + len(weights)),
        out_specs=[whole()] * 4,
        out_shape=[jax.ShapeDtypeStruct((2 * ROWS, HALF), f32)] * 2
        + [jax.ShapeDtypeStruct((2 * ROWS, LATE), bf16)] * 2,
        scratch_shapes=[
            VMEM((2 * ROWS, Q_WIDTH), bf16),
            VMEM((2 * ROWS, Q_WIDTH), bf16),
            VMEM((Q_WIDTH, HALF), bf16),
            VMEM((Q_WIDTH, HALF), bf16),
            pltpu.SemaphoreType.DMA((2,)),
        ],
        compiler_params=HUGE,
        cost_estimate=BRIEF,
    )(place, *outs, *weights)


def lanes_of(value):
    total = value[:, :128]
    for k in range(1, value.shape[1] // 128):
        total = total + value[:, k * 128 : (k + 1) * 128]
    return total


def project_last_kernel(
    place_ref, rows_p, rows_r, o2p, o2e, y_p, y_r, mine_ref, theirs_ref, after,
    y_ref, stats_ref, late_p, late_r, sums,
):
    j = pl.program_id(0)

    @pl.when(j == 0)
    def _():
        sums[...] = jnp.zeros_like(sums)
        for late in (late_p, late_r):
            late[SHARD:, :] = jnp.zeros((LATE - SHARD, WIDE), bf16)

    late_p[:SHARD, :] = o2p[...]
    late_r[:SHARD, :] = o2e[...]

    target = jnp.concatenate([mine_ref[...], theirs_ref[...]], axis=0).astype(f32)
    y = y_p[...] + dot(rows_p[...], late_p[...])
    y_ref[...] = y
    sums[0] += lanes_of(y * y)
    sums[1] += lanes_of(y * target)
    y = y_r[...] + dot(rows_r[...], late_r[...])
    sums[2] += lanes_of(y * y)
    sums[3] += lanes_of(y * target)

    @pl.when(j == HALF // WIDE - 1)
    def _():
        lane = lax.broadcasted_iota(jnp.int32, (2 * ROWS, 128), 1)
        stats = jnp.zeros((2 * ROWS, 128), f32)
        for k in range(4):
            stats = jnp.where(lane == k, jnp.sum(sums[k], axis=1, keepdims=True), stats)
        stats_ref[...] = stats


def project_last(place, parts, weights, target, after):
    steps = HALF // WIDE
    chunk = lambda rows: pl.BlockSpec((rows, WIDE), lambda j, place: (0, j))
    fixed = lambda width: pl.BlockSpec((2 * ROWS, width), lambda j, place: (0, 0))
    y_p, y_r, rows_p, rows_r = parts
    return pl.pallas_call(
        project_last_kernel,
        grid_spec=pltpu.PrefetchScalarGridSpec(
            num_scalar_prefetch=1,
            grid=(steps,),
            in_specs=[fixed(LATE)] * 2
            + [chunk(SHARD)] * 2
            + [chunk(2 * ROWS)] * 2
            + [
                pl.BlockSpec((ROWS, WIDE), lambda j, place: (0, TARGET_AT // WIDE + place[2] * steps + j)),
                pl.BlockSpec((ROWS, WIDE), lambda j, place: (0, TARGET_AT // WIDE + (1 - place[2]) * steps + j)),
                in_place(),
            ],
            out_specs=[chunk(2 * ROWS), fixed(128)],
            scratch_shapes=[
                VMEM((LATE, WIDE), bf16),
                VMEM((LATE, WIDE), bf16),
                VMEM((4, 2 * ROWS, 128), f32),
            ],
        ),
        out_shape=[
            jax.ShapeDtypeStruct((2 * ROWS, HALF), f32),
            jax.ShapeDtypeStruct((2 * ROWS, 128), f32),
        ],
        compiler_params=HUGE,
        cost_estimate=pl.CostEstimate(
            flops=2 * ROWS * Q_WIDTH * HALF, bytes_accessed=10 << 20, transcendentals=0
        ),
    )(place, rows_p, rows_r, *weights, y_p, y_r, target, target, after)


def gradient_kernel(
    place_ref, own_ref, other_ref, y_ref, stats_ref, more_ref, mine_ref, theirs_ref, facts_ref,
    a0, a1, a2, a3, b0, b1, b2, b3, rows, grad, terms, y, sems, first_out, second_out, out_sems,
):
    y_at, z = place_ref[0], place_ref[3]
    fetch = []
    for side, source in enumerate((own_ref, other_ref)):
        part = pl.ds(side * ROWS, ROWS)
        fetch.append(pltpu.make_async_copy(y_ref.at[part, :], y.at[part, :], sems.at[side]))
        fetch.append(pltpu.make_async_copy(source, rows.at[part, :], sems.at[2]))
    for copy in (fetch[0], fetch[2], fetch[1], fetch[3]):
        copy.start()
    row = lax.broadcasted_iota(jnp.int32, (ROWS, 1), 0)
    for side in range(2):
        here = slice(side * ROWS, (side + 1) * ROWS)
        there = slice((1 - side) * ROWS, (2 - side) * ROWS)
        stats = stats_ref[here, :] + more_ref[there, :]
        policy_squares, policy_products = stats[:, 0:1], stats[:, 1:2]
        reference_squares, reference_products = stats[:, 2:3], stats[:, 3:4]
        one, two = 2 * side, 2 * side + 1
        early = row.astype(f32) < facts_ref[4 + one : 5 + one, 0:1]
        length = jnp.where(early, facts_ref[4 + one : 5 + one, 0:1], facts_ref[4 + two : 5 + two, 0:1])
        advantage = jnp.where(early, facts_ref[one : one + 1, 0:1], facts_ref[two : two + 1, 0:1])
        policy_norm = jnp.sqrt(policy_squares / D_OUT + norm_epsilon)
        reference_norm = jnp.sqrt(reference_squares / D_OUT + norm_epsilon)
        policy_self = policy_squares / (policy_norm * policy_norm)
        policy_cross = policy_products / policy_norm
        reference_self = reference_squares / (reference_norm * reference_norm)
        reference_cross = reference_products / reference_norm
        gain = ((policy_self - reference_self) - 2.0 * (policy_cross - reference_cross)) * (
            1.0 / (4.0 * math.sqrt(D_OUT))
        )
        weight = (advantage - kl_weight * (1.0 - jnp.exp(gain))) / length
        along = (policy_self - policy_cross) / D_OUT
        scale = weight / policy_norm
        slope = scale * (1.0 - along) / policy_norm
        target = (mine_ref if side == 0 else theirs_ref)[...].astype(f32)
        fetch[2 * side].wait()
        grad[here, :] = (y[here, :] * slope - target * scale).astype(bf16)

    fetch[1].wait()
    fetch[3].wait()
    copies = []

    def give(source, out, at):
        copies.append(pltpu.make_async_copy(source, out, out_sems.at[at]))
        copies[-1].start()

    for d, out in enumerate((a0, a1, a2, a3)):
        at = lax.rem(z + d, 4)
        term = outer(rows[:, pl.ds(pl.multiple_of(at * PIECE, 128), PIECE)], grad[...])
        first_out[d] = term[:, :PIECE]
        give(first_out.at[d], out, d)
        terms[...] = term[:, PIECE:].reshape(2, 4, 80, PIECE)
        for k, second in enumerate((b0, b1, b2, b3)):
            here = pl.ds(2 * at, 2)
            second_out[k, here] = terms[:, lax.rem(y_at + k, 4)]
            give(second_out.at[k, here], second.at[here], 4 + 4 * d + k)
    for copy in copies:
        copy.wait()


def outer(rows, grad):
    return lax.dot_general(rows, grad, (((0,), (0,)), ((), ())), preferred_element_type=f32).astype(bf16)


def gradient(place, own, other, y, stats, more, target, facts):
    pieces = pl.pallas_call(
        gradient_kernel,
        grid_spec=pltpu.PrefetchScalarGridSpec(
            num_scalar_prefetch=1,
            grid=(1,),
            in_specs=[in_place()] * 3
            + [pl.BlockSpec((2 * ROWS, 128), lambda i, place: (0, 0))] * 2
            + [
                pl.BlockSpec((ROWS, HALF), lambda i, place: (0, TARGET_AT // HALF + place[2])),
                pl.BlockSpec((ROWS, HALF), lambda i, place: (0, TARGET_AT // HALF + 1 - place[2])),
                pl.BlockSpec((8, 128), lambda i, place: (0, 0)),
            ],
            out_specs=[in_place()] * 8,
            scratch_shapes=[
                VMEM((2 * ROWS, Q_WIDTH), bf16),
                VMEM((2 * ROWS, HALF), bf16),
                VMEM((2, 4, 80, PIECE), bf16),
                VMEM((2 * ROWS, HALF), f32),
                pltpu.SemaphoreType.DMA((3,)),
                VMEM((4, PIECE, PIECE), bf16),
                VMEM((4, 8, 80, PIECE), bf16),
                pltpu.SemaphoreType.DMA((20,)),
            ],
        ),
        out_shape=[jax.ShapeDtypeStruct((PIECE, PIECE), bf16)] * 4
        + [jax.ShapeDtypeStruct((8, 80, PIECE), bf16)] * 4,
        compiler_params=HUGE,
        cost_estimate=pl.CostEstimate(
            flops=4 * ROWS * Q_WIDTH * HALF, bytes_accessed=16 << 20, transcendentals=0
        ),
    )(place, own, other, y, stats, more, target, target, facts)
    return pieces[:4], pieces[4:]


def total_of(refs, index):
    total = refs[0][index].astype(f32)
    for ref in refs[1:]:
        total = total + ref[index].astype(f32)
    return total


def sum_kernel(axis, place_at, place_ref, *refs):
    parts, outs = refs[:4], refs[4:]
    own = place_ref[place_at]
    for d, out in enumerate(outs):
        at = lax.rem(own + d, 4)
        index = (slice(None), at) if axis == 1 else (at,)
        out[...] = total_of(parts, index).astype(bf16)


def sum_blocks(place, parts, axis, place_at):
    shape = (2, 80, PIECE)
    return pl.pallas_call(
        functools.partial(sum_kernel, axis, place_at),
        in_specs=[scalars()] + [whole()] * 4,
        out_specs=[whole()] * 4,
        out_shape=[jax.ShapeDtypeStruct(shape, bf16)] * 4,
        compiler_params=SMALL,
        cost_estimate=pl.CostEstimate(flops=4 << 20, bytes_accessed=5 << 20, transcendentals=0),
    )(place, *parts)


def last_sum_kernel(place_ref, *refs):
    first, second, keep, send = refs[:4], refs[4:8], refs[8], refs[9]
    xh = place_ref[4]
    for out, at in ((keep, xh), (send, 1 - xh)):
        out[:, :PIECE] = total_of(first, (at,)).astype(bf16)
        out[:, PIECE:] = total_of(second, (at,)).astype(bf16)


def last_sum(place, first, second):
    return pl.pallas_call(
        last_sum_kernel,
        in_specs=[scalars()] + [whole()] * 8,
        out_specs=[whole()] * 2,
        out_shape=[jax.ShapeDtypeStruct((80, HALF), bf16)] * 2,
        compiler_params=SMALL,
    )(place, *first, *second)


def step_kernel(
    place_ref, square_ref, mine_ref, theirs_ref, weight_ref, ema_ref,
    update_out, moved_out, next_out, update, moved, after, sems,
):
    scale = lax.rsqrt(square_ref[0:1, 0:1] / (Q_WIDTH * D_OUT) + norm_epsilon)
    y_at, c = place_ref[0], place_ref[2]
    copies = []
    for d in range(4):
        rows = pl.ds(pl.multiple_of(lax.rem(y_at + d, 4) * 80, 16), 80)
        for side, grad_ref in ((c, mine_ref), (1 - c, theirs_ref)):
            lanes = pl.ds(pl.multiple_of(side * HALF, 128), HALF)
            step = grad_ref[d].astype(f32) * scale
            weight = weight_ref[rows, lanes].astype(f32) - step_size * step
            update[rows, lanes] = step
            moved[rows, lanes] = weight.astype(bf16)
            after[rows, lanes] = ema_decay * ema_ref[rows, lanes] + (1.0 - ema_decay) * weight
        for k, (source, out) in enumerate(((update, update_out), (moved, moved_out), (after, next_out))):
            copies.append(pltpu.make_async_copy(source.at[rows, :], out.at[rows, :], sems.at[k, d]))
            copies[-1].start()
    for copy in copies:
        copy.wait()


def square_kernel(mine_ref, theirs_ref, out_ref):
    def block(d):
        mine, theirs = mine_ref[d].astype(f32), theirs_ref[d].astype(f32)
        return jnp.sum(mine * mine, keepdims=True) + jnp.sum(theirs * theirs, keepdims=True)

    total = (block(0) + block(2)) + (block(1) + block(3))
    out_ref[...] = jnp.broadcast_to(total, (8, 128))


def take_step(place, square_sum, mine, theirs, policy_weight, ema_weight):
    return pl.pallas_call(
        step_kernel,
        in_specs=[scalars()] + [whole()] * 5,
        out_specs=[in_place()] * 3,
        out_shape=[
            jax.ShapeDtypeStruct((SHARD, D_OUT), f32),
            jax.ShapeDtypeStruct((SHARD, D_OUT), bf16),
            jax.ShapeDtypeStruct((SHARD, D_OUT), f32),
        ],
        scratch_shapes=[
            VMEM((SHARD, D_OUT), f32),
            VMEM((SHARD, D_OUT), bf16),
            VMEM((SHARD, D_OUT), f32),
            pltpu.SemaphoreType.DMA((3, 4)),
        ],
        compiler_params=pltpu.CompilerParams(vmem_limit_bytes=24 * 1024 * 1024),
    )(place, square_sum, mine, theirs, policy_weight, ema_weight)


def local(
    q_policy,
    kv_policy,
    q_reference,
    kv_reference,
    target,
    send_slot,
    lengths,
    rewards,
    group_ids,
    policy_weight,
    ema_weight,
):
    place = jnp.stack([lax.axis_index(name) for name in EVERY]).astype(jnp.int32)
    c = place[2]
    send = lax.ppermute

    X = ("xl", "xh")

    def half(weight):
        return lax.dynamic_slice_in_dim(weight, c * HALF, HALF, 1).astype(bf16)

    w0 = jnp.concatenate([half(policy_weight), half(ema_weight)], axis=0)
    sm, sp, o0 = send(w0, "z", ring(1)), send(w0, "z", ring(-1)), send(w0, X, ACROSS)
    s2, op, om = send(sm, "z", ring(1)), send(o0, "z", ring(-1)), send(sm, X, ACROSS)
    late_p, late_e = halves(s2, om)
    o2p, o2e = send(late_p, X, ACROSS), send(late_e, "z", ring(1))

    exchange = functools.partial(lax.all_to_all, axis_name=DP, split_axis=0, concat_axis=0, tiled=True)
    rows_policy = exchange(
        pack(
            pack_policy_kernel,
            FACTS_AT + 128,
            (send_slot, q_policy, kv_policy, target),
            small=(rewards, group_ids, lengths),
        )
    )
    packed = pack(
        functools.partial(pack_rows_kernel, Q_WIDTH), Q_WIDTH + 1024, (send_slot, q_reference, kv_reference)
    )
    rows_reference = exchange(hold(packed, (rows_policy, sm, sp, o0)))
    out_policy = attend(rows_policy, lengths, TARGET_AT + D_OUT)
    other_policy = send(out_policy, "c", FLIP)
    facts = pl.pallas_call(
        facts_kernel,
        grid=(1,),
        in_specs=[pl.BlockSpec((ROWS, 128), lambda i: (0, FACTS_AT // 128))],
        out_specs=pl.BlockSpec((SPAN, 128), lambda i: (0, 0)),
        out_shape=jax.ShapeDtypeStruct((SPAN, 128), f32),
        compiler_params=SMALL,
    )(rows_policy)
    facts = jnp.concatenate([facts, send(facts, "xh", FLIP)], axis=0)
    advantages = pl.pallas_call(
        advantage_kernel,
        in_specs=[scalars()] + [whole()] * 4,
        out_specs=whole(),
        out_shape=jax.ShapeDtypeStruct((8, 128), f32),
        compiler_params=SMALL,
    )(place, facts, *[send(facts, "z", ring(d)) for d in (1, 2, 3)])
    out_reference = attend(rows_reference, lengths, Q_WIDTH)
    other_reference = send(out_reference, "c", FLIP)

    outs = (out_policy, other_policy, out_reference, other_reference)
    parts = project_most(place, outs, (w0, sm, sp, s2, o0, om, op, facts))
    y_policy, stats = project_last(place, parts, (o2p, o2e), rows_policy, advantages)
    more = send(stats, "c", FLIP)
    first, second = gradient(
        place, out_policy, other_policy, y_policy, stats, more, rows_policy, advantages
    )

    first = [first[0]] + [send(first[d], "z", ring(d)) for d in (1, 2, 3)]
    near = send(second[1], "y", ring(1))
    far = send(hold(second[2], (near,)), "y", ring(2))
    second = [second[0], near, far, send(second[3], "y", ring(3))]
    first = sum_blocks(place, [piece.reshape(2, 4, 80, PIECE) for piece in first], 1, 0)
    second = sum_blocks(place, [piece.reshape(4, 2, 80, PIECE) for piece in second], 0, 3)
    first = [first[0]] + [send(first[d], "y", ring(d)) for d in (1, 2, 3)]
    second = [second[0]] + [send(second[d], "z", ring(d)) for d in (1, 2, 3)]
    kept, given = last_sum(place, first, second)

    def add(one, two):
        return (one.astype(f32) + two.astype(f32)).astype(bf16)

    block = add(kept, send(given, X, ACROSS))
    block = add(block, send(block, "xl", FLIP))

    mine = jnp.stack([block] + [send(block, "y", ring(-d)) for d in (1, 2, 3)])
    theirs = send(mine, "c", FLIP)
    square = pl.pallas_call(
        square_kernel,
        in_specs=[whole()] * 2,
        out_specs=whole(),
        out_shape=jax.ShapeDtypeStruct((8, 128), f32),
        compiler_params=SMALL,
    )(mine, theirs)
    square = square + send(square, X, ACROSS)
    square = (square + send(square, "z", ring(2))) + (send(square, "z", ring(1)) + send(square, "z", ring(3)))
    return tuple(take_step(place, square, mine, theirs, policy_weight, ema_weight))


def solution(mesh):
    names = Mesh(mesh.devices.reshape(4, 2, 2, 4, 2), EVERY)
    rows, whole_rows = P(EVERY, None), P(EVERY)
    in_specs = (rows,) * 7 + (whole_rows,) * 2 + (P(FSDP, None),) * 2
    out_specs = (P(FSDP, None),) * 3
    return jax.shard_map(local, mesh=names, in_specs=in_specs, out_specs=out_specs, check_vma=False)
```

```python
import functools
import math

import jax
import jax.numpy as jnp
from jax import lax
from jax.experimental import pallas as pl
from jax.experimental.pallas import tpu as pltpu
from jax.sharding import Mesh
from jax.sharding import PartitionSpec as P

HEADS = 20
KV_HEADS = 4
HEAD_DIM = 128
D_OUT = 2560
GROUP = 8
Q_WIDTH = 2560
ROWS = 256
SPAN = 16
SHARD = 320
HALF = 1280
CHUNK = 256
WIDE = 640
PIECE = 640
LATE = 384
TARGET_AT = 2560
FACTS_AT = 6144

kl_weight = 0.1
step_size = 0.02
ema_decay = 0.95
std_floor = 0.6
norm_epsilon = 1e-06

bf16 = jnp.bfloat16
f32 = jnp.float32
VMEM = pltpu.VMEM
SMEM = pltpu.SMEM
BIG = pltpu.CompilerParams(vmem_limit_bytes=56 * 1024 * 1024)
HUGE = pltpu.CompilerParams(vmem_limit_bytes=63 * 1024 * 1024)
SMALL = pltpu.CompilerParams(vmem_limit_bytes=24 * 1024 * 1024)

BRIEF = pl.CostEstimate(flops=1, bytes_accessed=1, transcendentals=0)

DP = ("y", "xl", "c")
FSDP = ("z", "xh")
EVERY = DP + FSDP


def ring(step):
    return [(i, (i + step) % 4) for i in range(4)]


FLIP = [(0, 1), (1, 0)]
ACROSS = [(2, 1), (1, 2), (0, 3), (3, 0)]


def whole(shape=None):
    return pl.BlockSpec(memory_space=VMEM)


def scalars():
    return pl.BlockSpec(memory_space=SMEM)


def in_place():
    return pl.BlockSpec(memory_space=pl.ANY)


def dot(a, b):
    return jnp.dot(a, b, preferred_element_type=f32)


def one_hot_rows(slots_ref):
    return (lax.broadcasted_iota(jnp.int32, (ROWS, ROWS), 0) == slots_ref[...]).astype(bf16)


def pack_rows_kernel(kv_at, slots_ref, q_ref, kv_ref, *rest):
    out_ref = rest[-1]
    pick = one_hot_rows(slots_ref)
    out_ref[:, :Q_WIDTH] = dot(pick, q_ref[...]).astype(bf16)
    out_ref[:, kv_at : kv_at + 1024] = dot(pick, kv_ref[...]).astype(bf16)


def pack_policy_kernel(rewards_ref, ids_ref, lengths_ref, slots_ref, q_ref, kv_ref, target_ref, *rest):
    out_ref = rest[-1]
    pack_rows_kernel(TARGET_AT + D_OUT, slots_ref, q_ref, kv_ref, out_ref)
    rows = dot(one_hot_rows(slots_ref), target_ref[...]).astype(bf16)
    left, right = slice(TARGET_AT, TARGET_AT + HALF), slice(TARGET_AT + HALF, TARGET_AT + D_OUT)
    for pair in range(ROWS // (2 * SPAN)):
        top = pair * 2 * SPAN
        one, two = slice(top, top + SPAN), slice(top + SPAN, top + 2 * SPAN)
        out_ref[one, left] = rows[one, :HALF]
        out_ref[one, right] = rows[two, :HALF]
        out_ref[two, left] = rows[one, HALF:]
        out_ref[two, right] = rows[two, HALF:]
    lane = lax.broadcasted_iota(jnp.int32, (8, 128), 1)
    facts = jnp.zeros((8, 128), f32)
    given = (rewards_ref[0], rewards_ref[1], ids_ref[0], ids_ref[1], lengths_ref[0, 0], lengths_ref[0, 1])
    for k, fact in enumerate(given):
        facts = jnp.where(lane % 8 == k, fact.astype(f32), facts)
    high = facts.astype(bf16).astype(f32)
    middle = (facts - high).astype(bf16).astype(f32)
    low = facts - high - middle
    coded = jnp.where(lane < 8, high, jnp.where(lane < 16, middle, low))
    out_ref[:, FACTS_AT:] = jnp.broadcast_to(coded[0:1], (ROWS, 128)).astype(bf16)


def pack(kernel, width, operands, after=(), small=()):
    return pl.pallas_call(
        kernel,
        in_specs=[scalars()] * len(small) + [whole()] * len(operands) + [in_place()] * len(after),
        out_specs=whole(),
        out_shape=jax.ShapeDtypeStruct((ROWS, width), bf16),
        compiler_params=BIG,
        cost_estimate=BRIEF,
    )(*small, *operands, *after)


def gate_kernel(rows_ref, *rest):
    pass


def hold(rows, after):
    return pl.pallas_call(
        gate_kernel,
        in_specs=[in_place()] * (1 + len(after)),
        out_specs=in_place(),
        out_shape=jax.ShapeDtypeStruct(rows.shape, rows.dtype),
        input_output_aliases={0: 0},
    )(rows, *after)


def halves_kernel(first_ref, second_ref, policy_ref, averaged_ref):
    policy_ref[...] = first_ref[...]
    averaged_ref[...] = second_ref[...]


def halves(first, second):
    part = lambda at: pl.BlockSpec((SHARD, HALF), lambda i: (at, 0))
    return pl.pallas_call(
        halves_kernel,
        grid=(1,),
        in_specs=[part(0), part(1)],
        out_specs=[part(0)] * 2,
        out_shape=[jax.ShapeDtypeStruct((SHARD, HALF), bf16)] * 2,
        compiler_params=BIG,
    )(first, second)


def attention_kernel(lengths_ref, q_ref, k_ref, v_ref, *rest):
    out_ref = rest[-1]
    row = lax.broadcasted_iota(jnp.int32, (ROWS, ROWS), 0)
    column = lax.broadcasted_iota(jnp.int32, (ROWS, ROWS), 1)
    bound = lengths_ref[0, 0]
    allowed = (column <= row) & ((column >= bound) | (row < bound))
    keys, values = k_ref[...], v_ref[...]
    for head in range(HEADS // KV_HEADS):
        lanes = slice(head * HEAD_DIM, (head + 1) * HEAD_DIM)
        scores = lax.dot_general(
            q_ref[:, lanes], keys, (((1,), (1,)), ((), ())), preferred_element_type=f32
        ) * (1.0 / math.sqrt(HEAD_DIM))
        scores = jnp.where(allowed, scores, -1e30)
        weights = jnp.exp(scores - jnp.max(scores, axis=1, keepdims=True))
        shares = (weights / jnp.sum(weights, axis=1, keepdims=True)).astype(bf16)
        out_ref[:, lanes] = dot(shares, values).astype(bf16)


def attend(rows, lengths, kv_at, after=()):
    q_at, k_at, v_at = 0, kv_at, kv_at + 512
    width = Q_WIDTH // KV_HEADS
    return pl.pallas_call(
        attention_kernel,
        grid=(KV_HEADS,),
        in_specs=[
            scalars(),
            pl.BlockSpec((ROWS, width), lambda g: (0, q_at // width + g)),
            pl.BlockSpec((ROWS, HEAD_DIM), lambda g: (0, k_at // HEAD_DIM + g)),
            pl.BlockSpec((ROWS, HEAD_DIM), lambda g: (0, v_at // HEAD_DIM + g)),
        ]
        + [in_place()] * len(after),
        out_specs=pl.BlockSpec((ROWS, width), lambda g: (0, g)),
        out_shape=jax.ShapeDtypeStruct((ROWS, Q_WIDTH), bf16),
        compiler_params=BIG,
        cost_estimate=BRIEF,
    )(lengths, rows, rows, rows, *after)


def facts_kernel(coded_ref, out_ref):
    for block in range(ROWS // SPAN):
        coded = coded_ref[block * SPAN : (block + 1) * SPAN, :].astype(f32)[:8]
        facts = coded + pltpu.roll(coded, 128 - 8, 1) + pltpu.roll(coded, 128 - 16, 1)
        out_ref[block : block + 1, :] = facts[0:1]


def advantage_kernel(place_ref, one, two, three, four, out_ref):
    facts = jnp.concatenate([one[...], two[...], three[...], four[...]], axis=0)
    row = lax.broadcasted_iota(jnp.int32, facts.shape, 0)
    lane = lax.broadcasted_iota(jnp.int32, facts.shape, 1)
    ids = pltpu.roll(facts, 128 - 2, 1)
    chip = place_ref[0] * 4 + place_ref[1] * 2
    own, other = chip + place_ref[2], chip + 1 - place_ref[2]

    def fact(device, at):
        return jnp.sum(jnp.where((row == device) & (lane == at), facts, 0.0))

    for j in range(4):
        device, mine = (own, other)[j // 2], j % 2
        reward, group = fact(device, mine), fact(device, 2 + mine)
        held = jnp.where((lane < 2) & (ids == group), facts, 0.0)
        center = jnp.sum(held, keepdims=True) / GROUP
        second = jnp.sum(held * held, keepdims=True) / GROUP
        spread = jnp.maximum(jnp.sqrt(jnp.maximum(second - center * center, 0.0)), std_floor)
        out_ref[j : j + 1, :] = jnp.broadcast_to((reward - center) / spread, (1, 128))
        out_ref[4 + j : 5 + j, :] = jnp.full((1, 128), fact(device, 4 + mine), f32)


def project_most_kernel(
    place_ref, own_p, other_p, own_r, other_r, w0, sm, sp, s2, o0, om, op, after,
    y_p, y_r, late_p, late_r, rows_p, rows_r, weight_p, weight_r, sems,
):
    z, xh = place_ref[3], place_ref[4]
    here, there = xh, 1 - xh

    def place_of(dz, side):
        return pl.multiple_of((lax.rem(z + 4 + dz, 4) * 2 + side) * SHARD, 64)

    blocks = (
        (w0, 0, here), (sm, -1, here), (sp, 1, here), (s2, 2, here),
        (o0, 0, there), (om, -1, there), (op, 1, there),
    )
    copies = []
    for k, (own, other, rows, weight) in enumerate(
        ((own_p, other_p, rows_p, weight_p), (own_r, other_r, rows_r, weight_r))
    ):
        group = [
            pltpu.make_async_copy(own, rows.at[pl.ds(0, ROWS), :], sems.at[k]),
            pltpu.make_async_copy(other, rows.at[pl.ds(ROWS, ROWS), :], sems.at[k]),
        ]
        for block, dz, side in blocks:
            group.append(
                pltpu.make_async_copy(
                    block.at[pl.ds(k * SHARD, SHARD), :],
                    weight.at[pl.ds(place_of(dz, side), SHARD), :],
                    sems.at[k],
                )
            )
        for copy in group:
            copy.start()
        copies.append(group)
    for weight in (weight_p, weight_r):
        weight[pl.ds(place_of(2, there), SHARD), :] = jnp.zeros((SHARD, HALF), bf16)

    def run(rows, weight, out, late):
        def step(j, carry):
            at = pl.multiple_of(j * CHUNK, CHUNK)
            out[:, pl.ds(at, CHUNK)] = dot(rows[...], weight[:, pl.ds(at, CHUNK)])
            return carry

        lax.fori_loop(0, HALF // CHUNK, step, 0)
        part = rows[:, pl.ds(pl.multiple_of(lax.rem(z + 2, 4) * PIECE, 128), PIECE)].astype(f32)
        part = jnp.where(there == 0, part, pltpu.roll(part, PIECE - SHARD, 1))
        late[...] = part[:, :LATE].astype(bf16)

    for copy in copies[0]:
        copy.wait()
    run(rows_p, weight_p, y_p, late_p)
    for copy in copies[1]:
        copy.wait()
    run(rows_r, weight_r, y_r, late_r)


def project_most(place, outs, weights):
    return pl.pallas_call(
        project_most_kernel,
        in_specs=[scalars()] + [in_place()] * (len(outs) + len(weights)),
        out_specs=[whole()] * 4,
        out_shape=[jax.ShapeDtypeStruct((2 * ROWS, HALF), f32)] * 2
        + [jax.ShapeDtypeStruct((2 * ROWS, LATE), bf16)] * 2,
        scratch_shapes=[
            VMEM((2 * ROWS, Q_WIDTH), bf16),
            VMEM((2 * ROWS, Q_WIDTH), bf16),
            VMEM((Q_WIDTH, HALF), bf16),
            VMEM((Q_WIDTH, HALF), bf16),
            pltpu.SemaphoreType.DMA((2,)),
        ],
        compiler_params=HUGE,
        cost_estimate=BRIEF,
    )(place, *outs, *weights)


def lanes_of(value):
    total = value[:, :128]
    for k in range(1, value.shape[1] // 128):
        total = total + value[:, k * 128 : (k + 1) * 128]
    return total


def project_last_kernel(
    place_ref, rows_p, rows_r, o2p, o2e, y_p, y_r, mine_ref, theirs_ref, after,
    y_ref, stats_ref, late_p, late_r, sums,
):
    j = pl.program_id(0)

    @pl.when(j == 0)
    def _():
        sums[...] = jnp.zeros_like(sums)
        for late in (late_p, late_r):
            late[SHARD:, :] = jnp.zeros((LATE - SHARD, WIDE), bf16)

    late_p[:SHARD, :] = o2p[...]
    late_r[:SHARD, :] = o2e[...]

    target = jnp.concatenate([mine_ref[...], theirs_ref[...]], axis=0).astype(f32)
    y = y_p[...] + dot(rows_p[...], late_p[...])
    y_ref[...] = y
    sums[0] += lanes_of(y * y)
    sums[1] += lanes_of(y * target)
    y = y_r[...] + dot(rows_r[...], late_r[...])
    sums[2] += lanes_of(y * y)
    sums[3] += lanes_of(y * target)

    @pl.when(j == HALF // WIDE - 1)
    def _():
        lane = lax.broadcasted_iota(jnp.int32, (2 * ROWS, 128), 1)
        stats = jnp.zeros((2 * ROWS, 128), f32)
        for k in range(4):
            stats = jnp.where(lane == k, jnp.sum(sums[k], axis=1, keepdims=True), stats)
        stats_ref[...] = stats


def project_last(place, parts, weights, target, after):
    steps = HALF // WIDE
    chunk = lambda rows: pl.BlockSpec((rows, WIDE), lambda j, place: (0, j))
    fixed = lambda width: pl.BlockSpec((2 * ROWS, width), lambda j, place: (0, 0))
    y_p, y_r, rows_p, rows_r = parts
    return pl.pallas_call(
        project_last_kernel,
        grid_spec=pltpu.PrefetchScalarGridSpec(
            num_scalar_prefetch=1,
            grid=(steps,),
            in_specs=[fixed(LATE)] * 2
            + [chunk(SHARD)] * 2
            + [chunk(2 * ROWS)] * 2
            + [
                pl.BlockSpec((ROWS, WIDE), lambda j, place: (0, TARGET_AT // WIDE + place[2] * steps + j)),
                pl.BlockSpec((ROWS, WIDE), lambda j, place: (0, TARGET_AT // WIDE + (1 - place[2]) * steps + j)),
                in_place(),
            ],
            out_specs=[chunk(2 * ROWS), fixed(128)],
            scratch_shapes=[
                VMEM((LATE, WIDE), bf16),
                VMEM((LATE, WIDE), bf16),
                VMEM((4, 2 * ROWS, 128), f32),
            ],
        ),
        out_shape=[
            jax.ShapeDtypeStruct((2 * ROWS, HALF), f32),
            jax.ShapeDtypeStruct((2 * ROWS, 128), f32),
        ],
        compiler_params=HUGE,
        cost_estimate=pl.CostEstimate(
            flops=2 * ROWS * Q_WIDTH * HALF, bytes_accessed=10 << 20, transcendentals=0
        ),
    )(place, rows_p, rows_r, *weights, y_p, y_r, target, target, after)


def gradient_kernel(
    place_ref, own_ref, other_ref, y_ref, stats_ref, more_ref, mine_ref, theirs_ref, facts_ref,
    a0, a1, a2, a3, b0, b1, b2, b3, rows, grad, terms, y, sems, first_out, second_out, out_sems,
):
    y_at, z = place_ref[0], place_ref[3]
    fetch = []
    for side, source in enumerate((own_ref, other_ref)):
        part = pl.ds(side * ROWS, ROWS)
        fetch.append(pltpu.make_async_copy(y_ref.at[part, :], y.at[part, :], sems.at[side]))
        fetch.append(pltpu.make_async_copy(source, rows.at[part, :], sems.at[2]))
    for copy in (fetch[0], fetch[2], fetch[1], fetch[3]):
        copy.start()
    row = lax.broadcasted_iota(jnp.int32, (ROWS, 1), 0)
    for side in range(2):
        here = slice(side * ROWS, (side + 1) * ROWS)
        there = slice((1 - side) * ROWS, (2 - side) * ROWS)
        stats = stats_ref[here, :] + more_ref[there, :]
        policy_squares, policy_products = stats[:, 0:1], stats[:, 1:2]
        reference_squares, reference_products = stats[:, 2:3], stats[:, 3:4]
        one, two = 2 * side, 2 * side + 1
        early = row.astype(f32) < facts_ref[4 + one : 5 + one, 0:1]
        length = jnp.where(early, facts_ref[4 + one : 5 + one, 0:1], facts_ref[4 + two : 5 + two, 0:1])
        advantage = jnp.where(early, facts_ref[one : one + 1, 0:1], facts_ref[two : two + 1, 0:1])
        policy_norm = jnp.sqrt(policy_squares / D_OUT + norm_epsilon)
        reference_norm = jnp.sqrt(reference_squares / D_OUT + norm_epsilon)
        policy_self = policy_squares / (policy_norm * policy_norm)
        policy_cross = policy_products / policy_norm
        reference_self = reference_squares / (reference_norm * reference_norm)
        reference_cross = reference_products / reference_norm
        gain = ((policy_self - reference_self) - 2.0 * (policy_cross - reference_cross)) * (
            1.0 / (4.0 * math.sqrt(D_OUT))
        )
        weight = (advantage - kl_weight * (1.0 - jnp.exp(gain))) / length
        along = (policy_self - policy_cross) / D_OUT
        scale = weight / policy_norm
        slope = scale * (1.0 - along) / policy_norm
        target = (mine_ref if side == 0 else theirs_ref)[...].astype(f32)
        fetch[2 * side].wait()
        grad[here, :] = (y[here, :] * slope - target * scale).astype(bf16)

    fetch[1].wait()
    fetch[3].wait()
    copies = []

    def give(source, out, at):
        copies.append(pltpu.make_async_copy(source, out, out_sems.at[at]))
        copies[-1].start()

    for d, out in enumerate((a0, a1, a2, a3)):
        at = lax.rem(z + d, 4)
        term = outer(rows[:, pl.ds(pl.multiple_of(at * PIECE, 128), PIECE)], grad[...])
        first_out[d] = term[:, :PIECE]
        give(first_out.at[d], out, d)
        terms[...] = term[:, PIECE:].reshape(2, 4, 80, PIECE)
        for k, second in enumerate((b0, b1, b2, b3)):
            here = pl.ds(2 * at, 2)
            second_out[k, here] = terms[:, lax.rem(y_at + k, 4)]
            give(second_out.at[k, here], second.at[here], 4 + 4 * d + k)
    for copy in copies:
        copy.wait()


def outer(rows, grad):
    return lax.dot_general(rows, grad, (((0,), (0,)), ((), ())), preferred_element_type=f32).astype(bf16)


def gradient(place, own, other, y, stats, more, target, facts):
    pieces = pl.pallas_call(
        gradient_kernel,
        grid_spec=pltpu.PrefetchScalarGridSpec(
            num_scalar_prefetch=1,
            grid=(1,),
            in_specs=[in_place()] * 3
            + [pl.BlockSpec((2 * ROWS, 128), lambda i, place: (0, 0))] * 2
            + [
                pl.BlockSpec((ROWS, HALF), lambda i, place: (0, TARGET_AT // HALF + place[2])),
                pl.BlockSpec((ROWS, HALF), lambda i, place: (0, TARGET_AT // HALF + 1 - place[2])),
                pl.BlockSpec((8, 128), lambda i, place: (0, 0)),
            ],
            out_specs=[in_place()] * 8,
            scratch_shapes=[
                VMEM((2 * ROWS, Q_WIDTH), bf16),
                VMEM((2 * ROWS, HALF), bf16),
                VMEM((2, 4, 80, PIECE), bf16),
                VMEM((2 * ROWS, HALF), f32),
                pltpu.SemaphoreType.DMA((3,)),
                VMEM((4, PIECE, PIECE), bf16),
                VMEM((4, 8, 80, PIECE), bf16),
                pltpu.SemaphoreType.DMA((20,)),
            ],
        ),
        out_shape=[jax.ShapeDtypeStruct((PIECE, PIECE), bf16)] * 4
        + [jax.ShapeDtypeStruct((8, 80, PIECE), bf16)] * 4,
        compiler_params=HUGE,
        cost_estimate=pl.CostEstimate(
            flops=4 * ROWS * Q_WIDTH * HALF, bytes_accessed=16 << 20, transcendentals=0
        ),
    )(place, own, other, y, stats, more, target, target, facts)
    return pieces[:4], pieces[4:]


def total_of(refs, index):
    total = refs[0][index].astype(f32)
    for ref in refs[1:]:
        total = total + ref[index].astype(f32)
    return total


def sum_kernel(axis, place_at, place_ref, *refs):
    parts, outs = refs[:4], refs[4:]
    own = place_ref[place_at]
    for d, out in enumerate(outs):
        at = lax.rem(own + d, 4)
        index = (slice(None), at) if axis == 1 else (at,)
        out[...] = total_of(parts, index).astype(bf16)


def sum_blocks(place, parts, axis, place_at):
    shape = (2, 80, PIECE)
    return pl.pallas_call(
        functools.partial(sum_kernel, axis, place_at),
        in_specs=[scalars()] + [whole()] * 4,
        out_specs=[whole()] * 4,
        out_shape=[jax.ShapeDtypeStruct(shape, bf16)] * 4,
        compiler_params=SMALL,
        cost_estimate=pl.CostEstimate(flops=4 << 20, bytes_accessed=5 << 20, transcendentals=0),
    )(place, *parts)


def last_sum_kernel(place_ref, *refs):
    first, second, keep, send = refs[:4], refs[4:8], refs[8], refs[9]
    xh = place_ref[4]
    for out, at in ((keep, xh), (send, 1 - xh)):
        out[:, :PIECE] = total_of(first, (at,)).astype(bf16)
        out[:, PIECE:] = total_of(second, (at,)).astype(bf16)


def last_sum(place, first, second):
    return pl.pallas_call(
        last_sum_kernel,
        in_specs=[scalars()] + [whole()] * 8,
        out_specs=[whole()] * 2,
        out_shape=[jax.ShapeDtypeStruct((80, HALF), bf16)] * 2,
        compiler_params=SMALL,
    )(place, *first, *second)


def step_kernel(
    place_ref, square_ref, mine_ref, theirs_ref, weight_ref, ema_ref,
    update_out, moved_out, next_out, update, moved, after, sems,
):
    scale = lax.rsqrt(square_ref[0:1, 0:1] / (Q_WIDTH * D_OUT) + norm_epsilon)
    y_at, c = place_ref[0], place_ref[2]
    copies = []
    for d in range(4):
        rows = pl.ds(pl.multiple_of(lax.rem(y_at + d, 4) * 80, 16), 80)
        for side, grad_ref in ((c, mine_ref), (1 - c, theirs_ref)):
            lanes = pl.ds(pl.multiple_of(side * HALF, 128), HALF)
            step = grad_ref[d].astype(f32) * scale
            weight = weight_ref[rows, lanes].astype(f32) - step_size * step
            update[rows, lanes] = step
            moved[rows, lanes] = weight.astype(bf16)
            after[rows, lanes] = ema_decay * ema_ref[rows, lanes] + (1.0 - ema_decay) * weight
        for k, (source, out) in enumerate(((update, update_out), (moved, moved_out), (after, next_out))):
            copies.append(pltpu.make_async_copy(source.at[rows, :], out.at[rows, :], sems.at[k, d]))
            copies[-1].start()
    for copy in copies:
        copy.wait()


def square_kernel(mine_ref, theirs_ref, out_ref):
    def block(d):
        mine, theirs = mine_ref[d].astype(f32), theirs_ref[d].astype(f32)
        return jnp.sum(mine * mine, keepdims=True) + jnp.sum(theirs * theirs, keepdims=True)

    total = (block(0) + block(2)) + (block(1) + block(3))
    out_ref[...] = jnp.broadcast_to(total, (8, 128))


def take_step(place, square_sum, mine, theirs, policy_weight, ema_weight):
    return pl.pallas_call(
        step_kernel,
        in_specs=[scalars()] + [whole()] * 5,
        out_specs=[in_place()] * 3,
        out_shape=[
            jax.ShapeDtypeStruct((SHARD, D_OUT), f32),
            jax.ShapeDtypeStruct((SHARD, D_OUT), bf16),
            jax.ShapeDtypeStruct((SHARD, D_OUT), f32),
        ],
        scratch_shapes=[
            VMEM((SHARD, D_OUT), f32),
            VMEM((SHARD, D_OUT), bf16),
            VMEM((SHARD, D_OUT), f32),
            pltpu.SemaphoreType.DMA((3, 4)),
        ],
        compiler_params=pltpu.CompilerParams(vmem_limit_bytes=24 * 1024 * 1024),
    )(place, square_sum, mine, theirs, policy_weight, ema_weight)


def local(
    q_policy,
    kv_policy,
    q_reference,
    kv_reference,
    target,
    send_slot,
    lengths,
    rewards,
    group_ids,
    policy_weight,
    ema_weight,
):
    place = jnp.stack([lax.axis_index(name) for name in EVERY]).astype(jnp.int32)
    c = place[2]
    send = lax.ppermute

    X = ("xl", "xh")

    def half(weight):
        return lax.dynamic_slice_in_dim(weight, c * HALF, HALF, 1).astype(bf16)

    w0 = jnp.concatenate([half(policy_weight), half(ema_weight)], axis=0)
    sm, sp, o0 = send(w0, "z", ring(1)), send(w0, "z", ring(-1)), send(w0, X, ACROSS)
    s2, op, om = send(sm, "z", ring(1)), send(o0, "z", ring(-1)), send(sm, X, ACROSS)
    late_p, late_e = halves(s2, om)
    o2p, o2e = send(late_p, X, ACROSS), send(late_e, "z", ring(1))

    exchange = functools.partial(lax.all_to_all, axis_name=DP, split_axis=0, concat_axis=0, tiled=True)
    rows_policy = exchange(
        pack(
            pack_policy_kernel,
            FACTS_AT + 128,
            (send_slot, q_policy, kv_policy, target),
            small=(rewards, group_ids, lengths),
        )
    )
    packed = pack(
        functools.partial(pack_rows_kernel, Q_WIDTH), Q_WIDTH + 1024, (send_slot, q_reference, kv_reference)
    )
    rows_reference = exchange(hold(packed, (rows_policy, sm, sp, o0)))
    out_policy = attend(rows_policy, lengths, TARGET_AT + D_OUT)
    other_policy = send(out_policy, "c", FLIP)
    facts = pl.pallas_call(
        facts_kernel,
        grid=(1,),
        in_specs=[pl.BlockSpec((ROWS, 128), lambda i: (0, FACTS_AT // 128))],
        out_specs=pl.BlockSpec((SPAN, 128), lambda i: (0, 0)),
        out_shape=jax.ShapeDtypeStruct((SPAN, 128), f32),
        compiler_params=SMALL,
    )(rows_policy)
    facts = hold(facts, (out_policy,))
    facts = jnp.concatenate([facts, send(facts, "xh", FLIP)], axis=0)
    advantages = pl.pallas_call(
        advantage_kernel,
        in_specs=[scalars()] + [whole()] * 4,
        out_specs=whole(),
        out_shape=jax.ShapeDtypeStruct((8, 128), f32),
        compiler_params=SMALL,
    )(place, facts, *[send(facts, "z", ring(d)) for d in (1, 2, 3)])
    out_reference = attend(rows_reference, lengths, Q_WIDTH)
    other_reference = send(out_reference, "c", FLIP)

    outs = (out_policy, other_policy, out_reference, other_reference)
    parts = project_most(place, outs, (w0, sm, sp, s2, o0, om, op, facts))
    y_policy, stats = project_last(place, parts, (o2p, o2e), rows_policy, advantages)
    more = send(stats, "c", FLIP)
    first, second = gradient(
        place, out_policy, other_policy, y_policy, stats, more, rows_policy, advantages
    )

    first = [first[0]] + [send(first[d], "z", ring(d)) for d in (1, 2, 3)]
    near = send(second[1], "y", ring(1))
    far = send(hold(second[2], (near,)), "y", ring(2))
    second = [second[0], near, far, send(second[3], "y", ring(3))]
    first = sum_blocks(place, [piece.reshape(2, 4, 80, PIECE) for piece in first], 1, 0)
    second = sum_blocks(place, [piece.reshape(4, 2, 80, PIECE) for piece in second], 0, 3)
    first = [first[0]] + [send(first[d], "y", ring(d)) for d in (1, 2, 3)]
    second = [second[0]] + [send(second[d], "z", ring(d)) for d in (1, 2, 3)]
    kept, given = last_sum(place, first, second)

    def add(one, two):
        return (one.astype(f32) + two.astype(f32)).astype(bf16)

    block = add(kept, send(given, X, ACROSS))
    block = add(block, send(block, "xl", FLIP))

    mine = jnp.stack([block] + [send(block, "y", ring(-d)) for d in (1, 2, 3)])
    theirs = send(mine, "c", FLIP)
    square = pl.pallas_call(
        square_kernel,
        in_specs=[whole()] * 2,
        out_specs=whole(),
        out_shape=jax.ShapeDtypeStruct((8, 128), f32),
        compiler_params=SMALL,
    )(mine, theirs)
    square = square + send(square, X, ACROSS)
    square = (square + send(square, "z", ring(2))) + (send(square, "z", ring(1)) + send(square, "z", ring(3)))
    return tuple(take_step(place, square, mine, theirs, policy_weight, ema_weight))


def solution(mesh):
    names = Mesh(mesh.devices.reshape(4, 2, 2, 4, 2), EVERY)
    rows, whole_rows = P(EVERY, None), P(EVERY)
    in_specs = (rows,) * 7 + (whole_rows,) * 2 + (P(FSDP, None),) * 2
    out_specs = (P(FSDP, None),) * 3
    return jax.shard_map(local, mesh=names, in_specs=in_specs, out_specs=out_specs, check_vma=False)
```

```python
import functools
import math

import jax
import jax.numpy as jnp
from jax import lax
from jax.experimental import pallas as pl
from jax.experimental.pallas import tpu as pltpu
from jax.sharding import Mesh
from jax.sharding import PartitionSpec as P

HEADS = 20
KV_HEADS = 4
HEAD_DIM = 128
D_OUT = 2560
GROUP = 8
Q_WIDTH = 2560
ROWS = 256
SPAN = 16
SHARD = 320
HALF = 1280
CHUNK = 256
WIDE = 640
PIECE = 640
LATE = 384
TARGET_AT = 2560
FACTS_AT = 6144

kl_weight = 0.1
step_size = 0.02
ema_decay = 0.95
std_floor = 0.6
norm_epsilon = 1e-06

bf16 = jnp.bfloat16
f32 = jnp.float32
VMEM = pltpu.VMEM
SMEM = pltpu.SMEM
BIG = pltpu.CompilerParams(vmem_limit_bytes=56 * 1024 * 1024)
HUGE = pltpu.CompilerParams(vmem_limit_bytes=63 * 1024 * 1024)
SMALL = pltpu.CompilerParams(vmem_limit_bytes=24 * 1024 * 1024)

BRIEF = pl.CostEstimate(flops=1, bytes_accessed=1, transcendentals=0)

DP = ("y", "xl", "c")
FSDP = ("z", "xh")
EVERY = DP + FSDP


def ring(step):
    return [(i, (i + step) % 4) for i in range(4)]


FLIP = [(0, 1), (1, 0)]
ACROSS = [(2, 1), (1, 2), (0, 3), (3, 0)]


def whole(shape=None):
    return pl.BlockSpec(memory_space=VMEM)


def scalars():
    return pl.BlockSpec(memory_space=SMEM)


def in_place():
    return pl.BlockSpec(memory_space=pl.ANY)


def dot(a, b):
    return jnp.dot(a, b, preferred_element_type=f32)


def one_hot_rows(slots_ref):
    return (lax.broadcasted_iota(jnp.int32, (ROWS, ROWS), 0) == slots_ref[...]).astype(bf16)


def pack_rows_kernel(kv_at, slots_ref, q_ref, kv_ref, *rest):
    out_ref = rest[-1]
    pick = one_hot_rows(slots_ref)
    out_ref[:, :Q_WIDTH] = dot(pick, q_ref[...]).astype(bf16)
    out_ref[:, kv_at : kv_at + 1024] = dot(pick, kv_ref[...]).astype(bf16)


def pack_policy_kernel(rewards_ref, ids_ref, lengths_ref, slots_ref, q_ref, kv_ref, target_ref, *rest):
    out_ref = rest[-1]
    pack_rows_kernel(TARGET_AT + D_OUT, slots_ref, q_ref, kv_ref, out_ref)
    rows = dot(one_hot_rows(slots_ref), target_ref[...]).astype(bf16)
    left, right = slice(TARGET_AT, TARGET_AT + HALF), slice(TARGET_AT + HALF, TARGET_AT + D_OUT)
    for pair in range(ROWS // (2 * SPAN)):
        top = pair * 2 * SPAN
        one, two = slice(top, top + SPAN), slice(top + SPAN, top + 2 * SPAN)
        out_ref[one, left] = rows[one, :HALF]
        out_ref[one, right] = rows[two, :HALF]
        out_ref[two, left] = rows[one, HALF:]
        out_ref[two, right] = rows[two, HALF:]
    lane = lax.broadcasted_iota(jnp.int32, (8, 128), 1)
    facts = jnp.zeros((8, 128), f32)
    given = (rewards_ref[0], rewards_ref[1], ids_ref[0], ids_ref[1], lengths_ref[0, 0], lengths_ref[0, 1])
    for k, fact in enumerate(given):
        facts = jnp.where(lane % 8 == k, fact.astype(f32), facts)
    high = facts.astype(bf16).astype(f32)
    middle = (facts - high).astype(bf16).astype(f32)
    low = facts - high - middle
    coded = jnp.where(lane < 8, high, jnp.where(lane < 16, middle, low))
    out_ref[:, FACTS_AT:] = jnp.broadcast_to(coded[0:1], (ROWS, 128)).astype(bf16)


def pack(kernel, width, operands, after=(), small=()):
    return pl.pallas_call(
        kernel,
        in_specs=[scalars()] * len(small) + [whole()] * len(operands) + [in_place()] * len(after),
        out_specs=whole(),
        out_shape=jax.ShapeDtypeStruct((ROWS, width), bf16),
        compiler_params=BIG,
        cost_estimate=BRIEF,
    )(*small, *operands, *after)


def gate_kernel(rows_ref, *rest):
    pass


def hold(rows, after):
    return pl.pallas_call(
        gate_kernel,
        in_specs=[in_place()] * (1 + len(after)),
        out_specs=in_place(),
        out_shape=jax.ShapeDtypeStruct(rows.shape, rows.dtype),
        input_output_aliases={0: 0},
    )(rows, *after)


def halves_kernel(first_ref, second_ref, policy_ref, averaged_ref):
    policy_ref[...] = first_ref[...]
    averaged_ref[...] = second_ref[...]


def halves(first, second):
    part = lambda at: pl.BlockSpec((SHARD, HALF), lambda i: (at, 0))
    return pl.pallas_call(
        halves_kernel,
        grid=(1,),
        in_specs=[part(0), part(1)],
        out_specs=[part(0)] * 2,
        out_shape=[jax.ShapeDtypeStruct((SHARD, HALF), bf16)] * 2,
        compiler_params=BIG,
    )(first, second)


def attention_kernel(lengths_ref, q_ref, k_ref, v_ref, *rest):
    out_ref = rest[-1]
    row = lax.broadcasted_iota(jnp.int32, (ROWS, ROWS), 0)
    column = lax.broadcasted_iota(jnp.int32, (ROWS, ROWS), 1)
    bound = lengths_ref[0, 0]
    allowed = (column <= row) & ((column >= bound) | (row < bound))
    keys, values = k_ref[...], v_ref[...]
    for head in range(HEADS // KV_HEADS):
        lanes = slice(head * HEAD_DIM, (head + 1) * HEAD_DIM)
        scores = lax.dot_general(
            q_ref[:, lanes], keys, (((1,), (1,)), ((), ())), preferred_element_type=f32
        ) * (1.0 / math.sqrt(HEAD_DIM))
        scores = jnp.where(allowed, scores, -1e30)
        weights = jnp.exp(scores - jnp.max(scores, axis=1, keepdims=True))
        shares = (weights / jnp.sum(weights, axis=1, keepdims=True)).astype(bf16)
        out_ref[:, lanes] = dot(shares, values).astype(bf16)


def attend(rows, lengths, kv_at, after=()):
    q_at, k_at, v_at = 0, kv_at, kv_at + 512
    width = Q_WIDTH // KV_HEADS
    return pl.pallas_call(
        attention_kernel,
        grid=(KV_HEADS,),
        in_specs=[
            scalars(),
            pl.BlockSpec((ROWS, width), lambda g: (0, q_at // width + g)),
            pl.BlockSpec((ROWS, HEAD_DIM), lambda g: (0, k_at // HEAD_DIM + g)),
            pl.BlockSpec((ROWS, HEAD_DIM), lambda g: (0, v_at // HEAD_DIM + g)),
        ]
        + [in_place()] * len(after),
        out_specs=pl.BlockSpec((ROWS, width), lambda g: (0, g)),
        out_shape=jax.ShapeDtypeStruct((ROWS, Q_WIDTH), bf16),
        compiler_params=BIG,
        cost_estimate=BRIEF,
    )(lengths, rows, rows, rows, *after)


def facts_kernel(coded_ref, out_ref):
    for block in range(ROWS // SPAN):
        coded = coded_ref[block * SPAN : (block + 1) * SPAN, :].astype(f32)[:8]
        facts = coded + pltpu.roll(coded, 128 - 8, 1) + pltpu.roll(coded, 128 - 16, 1)
        out_ref[block : block + 1, :] = facts[0:1]


def advantage_kernel(place_ref, one, two, three, four, out_ref):
    facts = jnp.concatenate([one[...], two[...], three[...], four[...]], axis=0)
    row = lax.broadcasted_iota(jnp.int32, facts.shape, 0)
    lane = lax.broadcasted_iota(jnp.int32, facts.shape, 1)
    ids = pltpu.roll(facts, 128 - 2, 1)
    chip = place_ref[0] * 4 + place_ref[1] * 2
    own, other = chip + place_ref[2], chip + 1 - place_ref[2]

    def fact(device, at):
        return jnp.sum(jnp.where((row == device) & (lane == at), facts, 0.0))

    for j in range(4):
        device, mine = (own, other)[j // 2], j % 2
        reward, group = fact(device, mine), fact(device, 2 + mine)
        held = jnp.where((lane < 2) & (ids == group), facts, 0.0)
        center = jnp.sum(held, keepdims=True) / GROUP
        second = jnp.sum(held * held, keepdims=True) / GROUP
        spread = jnp.maximum(jnp.sqrt(jnp.maximum(second - center * center, 0.0)), std_floor)
        out_ref[j : j + 1, :] = jnp.broadcast_to((reward - center) / spread, (1, 128))
        out_ref[4 + j : 5 + j, :] = jnp.full((1, 128), fact(device, 4 + mine), f32)


def project_most_kernel(
    place_ref, own_p, other_p, own_r, other_r, w0, sm, sp, s2, o0, om, op, after,
    y_p, y_r, late_p, late_r, rows_p, rows_r, weight_p, weight_r, sems,
):
    z, xh = place_ref[3], place_ref[4]
    here, there = xh, 1 - xh

    def place_of(dz, side):
        return pl.multiple_of((lax.rem(z + 4 + dz, 4) * 2 + side) * SHARD, 64)

    blocks = (
        (w0, 0, here), (sm, -1, here), (sp, 1, here), (s2, 2, here),
        (o0, 0, there), (om, -1, there), (op, 1, there),
    )
    copies = []
    for k, (own, other, rows, weight) in enumerate(
        ((own_p, other_p, rows_p, weight_p), (own_r, other_r, rows_r, weight_r))
    ):
        group = [
            pltpu.make_async_copy(own, rows.at[pl.ds(0, ROWS), :], sems.at[k]),
            pltpu.make_async_copy(other, rows.at[pl.ds(ROWS, ROWS), :], sems.at[k]),
        ]
        for block, dz, side in blocks:
            group.append(
                pltpu.make_async_copy(
                    block.at[pl.ds(k * SHARD, SHARD), :],
                    weight.at[pl.ds(place_of(dz, side), SHARD), :],
                    sems.at[k],
                )
            )
        for copy in group:
            copy.start()
        copies.append(group)
    for weight in (weight_p, weight_r):
        weight[pl.ds(place_of(2, there), SHARD), :] = jnp.zeros((SHARD, HALF), bf16)

    def run(rows, weight, out, late):
        def step(j, carry):
            at = pl.multiple_of(j * CHUNK, CHUNK)
            out[:, pl.ds(at, CHUNK)] = dot(rows[...], weight[:, pl.ds(at, CHUNK)])
            return carry

        lax.fori_loop(0, HALF // CHUNK, step, 0)
        part = rows[:, pl.ds(pl.multiple_of(lax.rem(z + 2, 4) * PIECE, 128), PIECE)].astype(f32)
        part = jnp.where(there == 0, part, pltpu.roll(part, PIECE - SHARD, 1))
        late[...] = part[:, :LATE].astype(bf16)

    for copy in copies[0]:
        copy.wait()
    run(rows_p, weight_p, y_p, late_p)
    for copy in copies[1]:
        copy.wait()
    run(rows_r, weight_r, y_r, late_r)


def project_most(place, outs, weights):
    return pl.pallas_call(
        project_most_kernel,
        in_specs=[scalars()] + [in_place()] * (len(outs) + len(weights)),
        out_specs=[whole()] * 4,
        out_shape=[jax.ShapeDtypeStruct((2 * ROWS, HALF), f32)] * 2
        + [jax.ShapeDtypeStruct((2 * ROWS, LATE), bf16)] * 2,
        scratch_shapes=[
            VMEM((2 * ROWS, Q_WIDTH), bf16),
            VMEM((2 * ROWS, Q_WIDTH), bf16),
            VMEM((Q_WIDTH, HALF), bf16),
            VMEM((Q_WIDTH, HALF), bf16),
            pltpu.SemaphoreType.DMA((2,)),
        ],
        compiler_params=HUGE,
        cost_estimate=BRIEF,
    )(place, *outs, *weights)


def lanes_of(value):
    total = value[:, :128]
    for k in range(1, value.shape[1] // 128):
        total = total + value[:, k * 128 : (k + 1) * 128]
    return total


def project_last_kernel(
    place_ref, rows_p, rows_r, o2p, o2e, y_p, y_r, mine_ref, theirs_ref, after,
    y_ref, stats_ref, late_p, late_r, sums,
):
    j = pl.program_id(0)

    @pl.when(j == 0)
    def _():
        sums[...] = jnp.zeros_like(sums)
        for late in (late_p, late_r):
            late[SHARD:, :] = jnp.zeros((LATE - SHARD, WIDE), bf16)

    late_p[:SHARD, :] = o2p[...]
    late_r[:SHARD, :] = o2e[...]

    target = jnp.concatenate([mine_ref[...], theirs_ref[...]], axis=0).astype(f32)
    y = y_p[...] + dot(rows_p[...], late_p[...])
    y_ref[...] = y
    sums[0] += lanes_of(y * y)
    sums[1] += lanes_of(y * target)
    y = y_r[...] + dot(rows_r[...], late_r[...])
    sums[2] += lanes_of(y * y)
    sums[3] += lanes_of(y * target)

    @pl.when(j == HALF // WIDE - 1)
    def _():
        lane = lax.broadcasted_iota(jnp.int32, (2 * ROWS, 128), 1)
        stats = jnp.zeros((2 * ROWS, 128), f32)
        for k in range(4):
            stats = jnp.where(lane == k, jnp.sum(sums[k], axis=1, keepdims=True), stats)
        stats_ref[...] = stats


def project_last(place, parts, weights, target, after):
    steps = HALF // WIDE
    chunk = lambda rows: pl.BlockSpec((rows, WIDE), lambda j, place: (0, j))
    fixed = lambda width: pl.BlockSpec((2 * ROWS, width), lambda j, place: (0, 0))
    y_p, y_r, rows_p, rows_r = parts
    return pl.pallas_call(
        project_last_kernel,
        grid_spec=pltpu.PrefetchScalarGridSpec(
            num_scalar_prefetch=1,
            grid=(steps,),
            in_specs=[fixed(LATE)] * 2
            + [chunk(SHARD)] * 2
            + [chunk(2 * ROWS)] * 2
            + [
                pl.BlockSpec((ROWS, WIDE), lambda j, place: (0, TARGET_AT // WIDE + place[2] * steps + j)),
                pl.BlockSpec((ROWS, WIDE), lambda j, place: (0, TARGET_AT // WIDE + (1 - place[2]) * steps + j)),
                in_place(),
            ],
            out_specs=[chunk(2 * ROWS), fixed(128)],
            scratch_shapes=[
                VMEM((LATE, WIDE), bf16),
                VMEM((LATE, WIDE), bf16),
                VMEM((4, 2 * ROWS, 128), f32),
            ],
        ),
        out_shape=[
            jax.ShapeDtypeStruct((2 * ROWS, HALF), f32),
            jax.ShapeDtypeStruct((2 * ROWS, 128), f32),
        ],
        compiler_params=HUGE,
        cost_estimate=pl.CostEstimate(
            flops=2 * ROWS * Q_WIDTH * HALF, bytes_accessed=10 << 20, transcendentals=0
        ),
    )(place, rows_p, rows_r, *weights, y_p, y_r, target, target, after)


def gradient_kernel(
    place_ref, own_ref, other_ref, y_ref, stats_ref, more_ref, mine_ref, theirs_ref, facts_ref,
    a0, a1, a2, a3, b0, b1, b2, b3, rows, grad, terms, y, sems, first_out, second_out, out_sems,
):
    y_at, z = place_ref[0], place_ref[3]
    fetch = []
    for side, source in enumerate((own_ref, other_ref)):
        part = pl.ds(side * ROWS, ROWS)
        fetch.append(pltpu.make_async_copy(y_ref.at[part, :], y.at[part, :], sems.at[side]))
        fetch.append(pltpu.make_async_copy(source, rows.at[part, :], sems.at[2]))
    for copy in (fetch[0], fetch[2], fetch[1], fetch[3]):
        copy.start()
    row = lax.broadcasted_iota(jnp.int32, (ROWS, 1), 0)
    for side in range(2):
        here = slice(side * ROWS, (side + 1) * ROWS)
        there = slice((1 - side) * ROWS, (2 - side) * ROWS)
        stats = stats_ref[here, :] + more_ref[there, :]
        policy_squares, policy_products = stats[:, 0:1], stats[:, 1:2]
        reference_squares, reference_products = stats[:, 2:3], stats[:, 3:4]
        one, two = 2 * side, 2 * side + 1
        early = row.astype(f32) < facts_ref[4 + one : 5 + one, 0:1]
        length = jnp.where(early, facts_ref[4 + one : 5 + one, 0:1], facts_ref[4 + two : 5 + two, 0:1])
        advantage = jnp.where(early, facts_ref[one : one + 1, 0:1], facts_ref[two : two + 1, 0:1])
        policy_norm = jnp.sqrt(policy_squares / D_OUT + norm_epsilon)
        reference_norm = jnp.sqrt(reference_squares / D_OUT + norm_epsilon)
        policy_self = policy_squares / (policy_norm * policy_norm)
        policy_cross = policy_products / policy_norm
        reference_self = reference_squares / (reference_norm * reference_norm)
        reference_cross = reference_products / reference_norm
        gain = ((policy_self - reference_self) - 2.0 * (policy_cross - reference_cross)) * (
            1.0 / (4.0 * math.sqrt(D_OUT))
        )
        weight = (advantage - kl_weight * (1.0 - jnp.exp(gain))) / length
        along = (policy_self - policy_cross) / D_OUT
        scale = weight / policy_norm
        slope = scale * (1.0 - along) / policy_norm
        target = (mine_ref if side == 0 else theirs_ref)[...].astype(f32)
        fetch[2 * side].wait()
        grad[here, :] = (y[here, :] * slope - target * scale).astype(bf16)

    fetch[1].wait()
    fetch[3].wait()
    copies = []

    def give(source, out, at):
        copies.append(pltpu.make_async_copy(source, out, out_sems.at[at]))
        copies[-1].start()

    for d, out in enumerate((a0, a1, a2, a3)):
        at = lax.rem(z + d, 4)
        term = outer(rows[:, pl.ds(pl.multiple_of(at * PIECE, 128), PIECE)], grad[...])
        first_out[d] = term[:, :PIECE]
        give(first_out.at[d], out, d)
        terms[...] = term[:, PIECE:].reshape(2, 4, 80, PIECE)
        for k, second in enumerate((b0, b1, b2, b3)):
            here = pl.ds(2 * at, 2)
            second_out[k, here] = terms[:, lax.rem(y_at + k, 4)]
            give(second_out.at[k, here], second.at[here], 4 + 4 * d + k)
    for copy in copies:
        copy.wait()


def outer(rows, grad):
    return lax.dot_general(rows, grad, (((0,), (0,)), ((), ())), preferred_element_type=f32).astype(bf16)


def gradient(place, own, other, y, stats, more, target, facts):
    pieces = pl.pallas_call(
        gradient_kernel,
        grid_spec=pltpu.PrefetchScalarGridSpec(
            num_scalar_prefetch=1,
            grid=(1,),
            in_specs=[in_place()] * 3
            + [pl.BlockSpec((2 * ROWS, 128), lambda i, place: (0, 0))] * 2
            + [
                pl.BlockSpec((ROWS, HALF), lambda i, place: (0, TARGET_AT // HALF + place[2])),
                pl.BlockSpec((ROWS, HALF), lambda i, place: (0, TARGET_AT // HALF + 1 - place[2])),
                pl.BlockSpec((8, 128), lambda i, place: (0, 0)),
            ],
            out_specs=[in_place()] * 8,
            scratch_shapes=[
                VMEM((2 * ROWS, Q_WIDTH), bf16),
                VMEM((2 * ROWS, HALF), bf16),
                VMEM((2, 4, 80, PIECE), bf16),
                VMEM((2 * ROWS, HALF), f32),
                pltpu.SemaphoreType.DMA((3,)),
                VMEM((4, PIECE, PIECE), bf16),
                VMEM((4, 8, 80, PIECE), bf16),
                pltpu.SemaphoreType.DMA((20,)),
            ],
        ),
        out_shape=[jax.ShapeDtypeStruct((PIECE, PIECE), bf16)] * 4
        + [jax.ShapeDtypeStruct((8, 80, PIECE), bf16)] * 4,
        compiler_params=HUGE,
        cost_estimate=pl.CostEstimate(
            flops=4 * ROWS * Q_WIDTH * HALF, bytes_accessed=16 << 20, transcendentals=0
        ),
    )(place, own, other, y, stats, more, target, target, facts)
    return pieces[:4], pieces[4:]


def total_of(refs, index):
    total = refs[0][index].astype(f32)
    for ref in refs[1:]:
        total = total + ref[index].astype(f32)
    return total


def sum_kernel(axis, place_at, place_ref, *refs):
    parts, outs = refs[:4], refs[4:]
    own = place_ref[place_at]
    for d, out in enumerate(outs):
        at = lax.rem(own + d, 4)
        index = (slice(None), at) if axis == 1 else (at,)
        out[...] = total_of(parts, index).astype(bf16)


def sum_blocks(place, parts, axis, place_at):
    shape = (2, 80, PIECE)
    return pl.pallas_call(
        functools.partial(sum_kernel, axis, place_at),
        in_specs=[scalars()] + [whole()] * 4,
        out_specs=[whole()] * 4,
        out_shape=[jax.ShapeDtypeStruct(shape, bf16)] * 4,
        compiler_params=SMALL,
        cost_estimate=pl.CostEstimate(flops=4 << 20, bytes_accessed=5 << 20, transcendentals=0),
    )(place, *parts)


def last_sum_kernel(place_ref, *refs):
    first, second, keep, send = refs[:4], refs[4:8], refs[8], refs[9]
    xh = place_ref[4]
    for out, at in ((keep, xh), (send, 1 - xh)):
        out[:, :PIECE] = total_of(first, (at,)).astype(bf16)
        out[:, PIECE:] = total_of(second, (at,)).astype(bf16)


def last_sum(place, first, second):
    return pl.pallas_call(
        last_sum_kernel,
        in_specs=[scalars()] + [whole()] * 8,
        out_specs=[whole()] * 2,
        out_shape=[jax.ShapeDtypeStruct((80, HALF), bf16)] * 2,
        compiler_params=SMALL,
    )(place, *first, *second)


def step_kernel(
    place_ref, square_ref, mine_ref, theirs_ref, weight_ref, ema_ref,
    update_out, moved_out, next_out, update, moved, after, sems,
):
    scale = lax.rsqrt(square_ref[0:1, 0:1] / (Q_WIDTH * D_OUT) + norm_epsilon)
    y_at, c = place_ref[0], place_ref[2]
    copies = []
    for d in range(4):
        rows = pl.ds(pl.multiple_of(lax.rem(y_at + d, 4) * 80, 16), 80)
        for side, grad_ref in ((c, mine_ref), (1 - c, theirs_ref)):
            lanes = pl.ds(pl.multiple_of(side * HALF, 128), HALF)
            step = grad_ref[d].astype(f32) * scale
            weight = weight_ref[rows, lanes].astype(f32) - step_size * step
            update[rows, lanes] = step
            moved[rows, lanes] = weight.astype(bf16)
            after[rows, lanes] = ema_decay * ema_ref[rows, lanes] + (1.0 - ema_decay) * weight
        for k, (source, out) in enumerate(((update, update_out), (moved, moved_out), (after, next_out))):
            copies.append(pltpu.make_async_copy(source.at[rows, :], out.at[rows, :], sems.at[k, d]))
            copies[-1].start()
    for copy in copies:
        copy.wait()


def square_kernel(mine_ref, theirs_ref, out_ref):
    def block(d):
        mine, theirs = mine_ref[d].astype(f32), theirs_ref[d].astype(f32)
        return jnp.sum(mine * mine, keepdims=True) + jnp.sum(theirs * theirs, keepdims=True)

    total = (block(0) + block(2)) + (block(1) + block(3))
    out_ref[...] = jnp.broadcast_to(total, (8, 128))


def take_step(place, square_sum, mine, theirs, policy_weight, ema_weight):
    return pl.pallas_call(
        step_kernel,
        in_specs=[scalars()] + [whole()] * 5,
        out_specs=[in_place()] * 3,
        out_shape=[
            jax.ShapeDtypeStruct((SHARD, D_OUT), f32),
            jax.ShapeDtypeStruct((SHARD, D_OUT), bf16),
            jax.ShapeDtypeStruct((SHARD, D_OUT), f32),
        ],
        scratch_shapes=[
            VMEM((SHARD, D_OUT), f32),
            VMEM((SHARD, D_OUT), bf16),
            VMEM((SHARD, D_OUT), f32),
            pltpu.SemaphoreType.DMA((3, 4)),
        ],
        compiler_params=pltpu.CompilerParams(vmem_limit_bytes=24 * 1024 * 1024),
    )(place, square_sum, mine, theirs, policy_weight, ema_weight)


def local(
    q_policy,
    kv_policy,
    q_reference,
    kv_reference,
    target,
    send_slot,
    lengths,
    rewards,
    group_ids,
    policy_weight,
    ema_weight,
):
    place = jnp.stack([lax.axis_index(name) for name in EVERY]).astype(jnp.int32)
    c = place[2]
    send = lax.ppermute

    X = ("xl", "xh")

    def half(weight):
        return lax.dynamic_slice_in_dim(weight, c * HALF, HALF, 1).astype(bf16)

    w0 = jnp.concatenate([half(policy_weight), half(ema_weight)], axis=0)
    sm, sp, o0 = send(w0, "z", ring(1)), send(w0, "z", ring(-1)), send(w0, X, ACROSS)
    s2, op, om = send(sm, "z", ring(1)), send(o0, "z", ring(-1)), send(sm, X, ACROSS)
    late_p, late_e = halves(s2, om)
    o2p, o2e = send(late_p, X, ACROSS), send(late_e, "z", ring(1))

    exchange = functools.partial(lax.all_to_all, axis_name=DP, split_axis=0, concat_axis=0, tiled=True)
    rows_policy = exchange(
        pack(
            pack_policy_kernel,
            FACTS_AT + 128,
            (send_slot, q_policy, kv_policy, target),
            small=(rewards, group_ids, lengths),
        )
    )
    packed = pack(
        functools.partial(pack_rows_kernel, Q_WIDTH), Q_WIDTH + 1024, (send_slot, q_reference, kv_reference)
    )
    facts = pl.pallas_call(
        facts_kernel,
        grid=(1,),
        in_specs=[pl.BlockSpec((ROWS, 128), lambda i: (0, FACTS_AT // 128))],
        out_specs=pl.BlockSpec((SPAN, 128), lambda i: (0, 0)),
        out_shape=jax.ShapeDtypeStruct((SPAN, 128), f32),
        compiler_params=SMALL,
    )(rows_policy)
    rows_reference = exchange(hold(packed, (facts, sm, sp, o0)))
    out_policy = attend(rows_policy, lengths, TARGET_AT + D_OUT)
    other_policy = send(out_policy, "c", FLIP)
    facts = hold(facts, (out_policy,))
    facts = jnp.concatenate([facts, send(facts, "xh", FLIP)], axis=0)
    advantages = pl.pallas_call(
        advantage_kernel,
        in_specs=[scalars()] + [whole()] * 4,
        out_specs=whole(),
        out_shape=jax.ShapeDtypeStruct((8, 128), f32),
        compiler_params=SMALL,
    )(place, facts, *[send(facts, "z", ring(d)) for d in (1, 2, 3)])
    out_reference = attend(rows_reference, lengths, Q_WIDTH)
    other_reference = send(out_reference, "c", FLIP)

    outs = (out_policy, other_policy, out_reference, other_reference)
    parts = project_most(place, outs, (w0, sm, sp, s2, o0, om, op, facts))
    y_policy, stats = project_last(place, parts, (o2p, o2e), rows_policy, advantages)
    more = send(stats, "c", FLIP)
    first, second = gradient(
        place, out_policy, other_policy, y_policy, stats, more, rows_policy, advantages
    )

    first = [first[0]] + [send(first[d], "z", ring(d)) for d in (1, 2, 3)]
    near = send(second[1], "y", ring(1))
    far = send(hold(second[2], (near,)), "y", ring(2))
    second = [second[0], near, far, send(second[3], "y", ring(3))]
    first = sum_blocks(place, [piece.reshape(2, 4, 80, PIECE) for piece in first], 1, 0)
    second = sum_blocks(place, [piece.reshape(4, 2, 80, PIECE) for piece in second], 0, 3)
    first = [first[0]] + [send(first[d], "y", ring(d)) for d in (1, 2, 3)]
    second = [second[0]] + [send(second[d], "z", ring(d)) for d in (1, 2, 3)]
    kept, given = last_sum(place, first, second)

    def add(one, two):
        return (one.astype(f32) + two.astype(f32)).astype(bf16)

    block = add(kept, send(given, X, ACROSS))
    block = add(block, send(block, "xl", FLIP))

    mine = jnp.stack([block] + [send(block, "y", ring(-d)) for d in (1, 2, 3)])
    theirs = send(mine, "c", FLIP)
    square = pl.pallas_call(
        square_kernel,
        in_specs=[whole()] * 2,
        out_specs=whole(),
        out_shape=jax.ShapeDtypeStruct((8, 128), f32),
        compiler_params=SMALL,
    )(mine, theirs)
    square = square + send(square, X, ACROSS)
    square = (square + send(square, "z", ring(2))) + (send(square, "z", ring(1)) + send(square, "z", ring(3)))
    return tuple(take_step(place, square, mine, theirs, policy_weight, ema_weight))


def solution(mesh):
    names = Mesh(mesh.devices.reshape(4, 2, 2, 4, 2), EVERY)
    rows, whole_rows = P(EVERY, None), P(EVERY)
    in_specs = (rows,) * 7 + (whole_rows,) * 2 + (P(FSDP, None),) * 2
    out_specs = (P(FSDP, None),) * 3
    return jax.shard_map(local, mesh=names, in_specs=in_specs, out_specs=out_specs, check_vma=False)
```
